128 devices in a mesh: row: 16 (over x, z), col: 8 (over y, core).
Axes of the slice: x: 4, y: 4, z: 4, core: 2. Of those that a mesh axis runs over, the one named last changes fastest.
Arguments:
- loader_rows: bfloat16 [256, 32, 6144], P('row', None, 'col'), may hold values from -6 to 6
- packing: int32 [256], P('row'), may hold values from 0 to 255, as said below
- segment_ids: int32 [16, 512], P('row'), may hold values from 0 to 5, never falling along the last dimension, each value on 1 to 160 neighbouring positions
- qkv_weight: bfloat16 [6144, 9216], P('row', 'col'), may hold values from -0.078125 to 0.078125
- gain_query: float32 [24, 128], P('col'), may hold values from 0.1 to 1.9
- gain_key: float32 [24, 128], P('col'), may hold values from 0.1 to 1.9
- out_grad: bfloat16 [8192, 3072], P('row', 'col'), may hold values from -6 to 6
Outputs:
- attn_out: bfloat16 [8192, 3072], P('row', 'col')
- grad_rows: bfloat16 [8192, 6144], P('row', 'col')
- grad_weight: bfloat16 [6144, 9216], P('row', 'col')
The draws below stay inside these ranges and needn't reach their ends.
Inputs may be any that keep to these rules, and one draw needn't show every extreme that they name: packing is a permutation of the 256 block slots. Block slots o * 16 to o * 16 + 15 belong to owner o; the 16 blocks of one loader device (aligned runs of 16 entries) send at most 2 blocks to one owner, and exactly 2 to some owner in every draw.
All inputs are finite; a program needn't handle non-finite values.
Results may differ from the reference program's by a relative error of at most 0.02.
Values may be sent and summed in bfloat16 or wider, within the bound.
No kernel may reach another device: no remote copies, remote signals or barrier semaphores. Data moves between devices by JAX's collectives and lax.ppermute only.
A program may use at most 192 MiB of HBM per device.

```python
import math
import jax
import jax.numpy as jnp
import numpy as np
from jax import lax

D = 6144
DH = 128
HEADS_W = 24
LEN = 512
IMAGES = 6
MOST_IMG = 160
BPL = 16
BLK = 32
SEQS = 16
ROWS = 8192
BLOCKS = 256
QKV_COLS = 9216
N_ROW = 16
N_COL = 8


def draw_packing(key, part):
    key = jax.random.fold_in(key, 11)
    owners = BLOCKS // BPL
    subkeys = jax.random.split(key, 5)
    offset_bit = jax.random.randint(subkeys[0], (), 0, 2)
    positions = jnp.arange(BPL)
    pair_index = (positions + offset_bit) // 2
    shifts = jax.random.permutation(subkeys[1], owners)[pair_index]
    relabel = jax.random.permutation(subkeys[2], owners)
    loader = jnp.arange(owners)
    owner_of = relabel[(loader[:, None] + shifts[None, :]) % owners]
    slot_table = jax.vmap(lambda sub: jax.random.permutation(sub, BPL))(jax.random.split(subkeys[3], owners))
    slot_of = slot_table[owner_of, positions[None, :]]
    targets = owner_of * BPL + slot_of
    shuffle = jax.vmap(lambda sub: jax.random.permutation(sub, BPL))(jax.random.split(subkeys[4], owners))
    result = jnp.take_along_axis(targets, shuffle, axis=1)
    return result.reshape(-1).astype(jnp.int32)


def level_of(key, dims, cuts, smallest, largest):
    level, own = 1.0, jax.random.fold_in(key, 6)
    for dim, blocks in cuts:
        draws = jnp.exp(jax.random.uniform(jax.random.fold_in(own, dim), (blocks,), jnp.float32, smallest / len(cuts), largest / len(cuts)))
        level = level * jnp.repeat(draws, dims[dim] // blocks).reshape([-1 if axis == dim else 1 for axis in range(len(dims))])
    return level


def profile(count, total, bound, lean):
    loads = [(1 << 20) // math.isqrt(grade ** lean) + 1 for grade in range(2, count + 1)]
    surplus, holding = total - bound - (count - 1), [1] * (count - 1)
    while surplus > 0:
        candidates = [i for i in range(count - 1) if holding[i] < bound]
        pool, budget = sum([loads[i] for i in candidates]), surplus
        for i in candidates:
            addition = min(bound - holding[i], max(1, budget * loads[i] // pool), surplus)
            holding[i] = holding[i] + addition
            surplus = surplus - addition
    return np.array([bound] + holding)


def uneven_parts(rng, amount, total, reach, lean):
    if amount == 2:
        one = jax.random.randint(rng, (), max(1, total - reach), min(reach, total - 1) + 1)
        return jnp.stack([one, total - one])
    lengths = jnp.asarray(profile(amount, total, reach, lean), jnp.int32)
    couples = (amount - 1) // 2
    source_of, receiver = lengths[1:1 + 2 * couples:2], lengths[2:2 + 2 * couples:2]
    margin = jnp.minimum(source_of - 1, reach - receiver)
    passed = jax.random.randint(jax.random.fold_in(rng, 1), (couples,), 0, 1 << 20) % (margin + 1)
    lengths = lengths.at[1:1 + 2 * couples:2].set(source_of - passed).at[2:2 + 2 * couples:2].set(receiver + passed)
    return lengths[jax.random.permutation(jax.random.fold_in(rng, 2), amount)]


def gaussian(stream_key, dims, deviation, bound, pieces=(), dtype=jnp.bfloat16):
    drawn = jax.random.normal(stream_key, dims, jnp.float32) * deviation
    if len(pieces) > 0:
        drawn = level_of(stream_key, dims, pieces, -0.22, 0.18) * drawn
    return jnp.clip(drawn, min=-bound, max=bound).astype(dtype)


def setup_inputs(seed: int = 0) -> dict:
    keys = jax.random.split(jax.random.key(seed), 8)
    return {
        "loader_rows": gaussian(keys[0], (BLOCKS, BLK, D), 1.0, 6.0, ((0, 16), (2, 8))),
        "packing": draw_packing(jax.random.fold_in(keys[7], 71), 0),
        "segment_ids": jax.vmap(lambda own: jnp.searchsorted(jnp.cumsum(uneven_parts(own, IMAGES, LEN, MOST_IMG, 2)), jnp.arange(LEN), side="right"))(jax.random.split(keys[2], SEQS)).reshape((SEQS, LEN)).astype(jnp.int32),
        "qkv_weight": gaussian(keys[3], (D, QKV_COLS), D ** -0.5, 0.078125, ((0, 16), (1, 8))),
        "gain_query": jnp.clip(1.0 + 0.18 * jax.random.normal(keys[4], (HEADS_W, DH), jnp.float32), 0.1, 1.9),
        "gain_key": jnp.clip(1.0 + 0.18 * jax.random.normal(keys[5], (HEADS_W, DH), jnp.float32), 0.1, 1.9),
        "out_grad": gaussian(keys[6], (ROWS, HEADS_W * DH), 1.0, 6.0, ((0, 16), (1, 8))),
    }


def normalize(values):
    centred = values - lax.optimization_barrier(jnp.mean(values, axis=-1, keepdims=True))
    inv_std = lax.rsqrt(lax.optimization_barrier(jnp.mean(centred * centred, axis=-1, keepdims=True)) + 1e-06)
    return (centred * inv_std, inv_std)

def norm_grad(upstream, normed, inv_std, gain):
    scaled = upstream * gain
    mean_one = lax.optimization_barrier(jnp.mean(scaled, axis=-1, keepdims=True))
    mean_two = lax.optimization_barrier(jnp.mean(scaled * normed, axis=-1, keepdims=True))
    return (scaled - mean_one - normed * mean_two) * inv_std

def attend(projected, gain_query, gain_key, segments, upstream):
    head_size = gain_query.shape[1]
    query_raw = projected[..., :head_size]
    key_raw = projected[..., head_size:2 * head_size]
    value_raw = projected[..., 2 * head_size:]
    query_hat, query_inv = normalize(query_raw)
    key_hat, key_inv = normalize(key_raw)
    query_normed = (query_hat * gain_query).astype(jnp.bfloat16).astype(jnp.float32)
    key_normed = (key_hat * gain_key).astype(jnp.bfloat16).astype(jnp.float32)
    value_half = value_raw.astype(jnp.bfloat16).astype(jnp.float32)
    factor = 1.0 / head_size ** 0.5
    scores = jnp.einsum('sqhe,skhe->shqk', query_normed, key_normed) * factor
    allowed = segments[:, None, :, None] == segments[:, None, None, :]
    exp_scores = jnp.where(allowed, jnp.exp(scores), 0.0)
    attn_probs = exp_scores / lax.optimization_barrier(jnp.sum(exp_scores, axis=-1, keepdims=True))
    probs_half = attn_probs.astype(jnp.bfloat16).astype(jnp.float32)
    output = jnp.einsum('shqk,skhe->sqhe', probs_half, value_half).astype(jnp.bfloat16)
    heads = gain_query.shape[0]
    out_heads = upstream.reshape(upstream.shape[0], upstream.shape[1], heads, head_size).astype(jnp.float32)
    grad_value = jnp.einsum('shqk,sqhe->skhe', probs_half, out_heads)
    grad_probs = jnp.einsum('sqhe,skhe->shqk', out_heads, value_half)
    inner = lax.optimization_barrier(jnp.sum(attn_probs * grad_probs, axis=-1, keepdims=True))
    grad_scores = (attn_probs * (grad_probs - inner) * factor).astype(jnp.bfloat16).astype(jnp.float32)
    grad_qn = jnp.einsum('shqk,skhe->sqhe', grad_scores, key_normed)
    grad_kn = jnp.einsum('shqk,sqhe->skhe', grad_scores, query_normed)
    grad_query = norm_grad(grad_qn, query_hat, query_inv, gain_query)
    grad_key = norm_grad(grad_kn, key_hat, key_inv, gain_key)
    grad_all = jnp.concatenate([grad_query, grad_key, grad_value], axis=-1).astype(jnp.bfloat16)
    return (output.reshape(output.shape[0], output.shape[1], heads * head_size), grad_all)

def reference(loader_rows, packing, segment_ids, qkv_weight, gain_query, gain_key, out_grad):
    packed = jnp.zeros_like(loader_rows).at[packing].set(loader_rows).reshape(ROWS, D)
    projected = jnp.dot(packed, qkv_weight, preferred_element_type=jnp.float32)
    projected = projected.reshape(SEQS, LEN, HEADS_W, 3 * DH)
    upstream = out_grad.reshape(SEQS, LEN, HEADS_W * DH)

    def one_sequence(items):
        proj_one, seg_one, up_one = items
        output, grad_all = attend(proj_one[None], gain_query, gain_key, seg_one[None], up_one[None])
        return (output[0], grad_all[0])
    outputs, grads = lax.map(one_sequence, (projected, segment_ids, upstream))
    attn_out = outputs.reshape(ROWS, HEADS_W * DH)
    grad_projected = grads.reshape(ROWS, QKV_COLS)
    group_cols = QKV_COLS // N_COL
    row_total = jnp.zeros((ROWS, D), jnp.float32)
    for group in range(N_COL):
        cols_grad = grad_projected[:, group * group_cols:(group + 1) * group_cols]
        cols_weight = qkv_weight[:, group * group_cols:(group + 1) * group_cols]
        piece = jnp.dot(cols_grad, cols_weight.T, preferred_element_type=jnp.float32).astype(jnp.bfloat16)
        row_total = row_total + lax.optimization_barrier(piece).astype(jnp.float32)
    owner_rows = ROWS // N_ROW
    weight_total = jnp.zeros((D, QKV_COLS), jnp.float32)
    for owner_index in range(N_ROW):
        rows_here = packed[owner_index * owner_rows:(owner_index + 1) * owner_rows]
        grads_here = grad_projected[owner_index * owner_rows:(owner_index + 1) * owner_rows]
        piece = jnp.dot(rows_here.T, grads_here, preferred_element_type=jnp.float32).astype(jnp.bfloat16)
        weight_total = weight_total + lax.optimization_barrier(piece).astype(jnp.float32)
    return (attn_out, row_total.astype(jnp.bfloat16), weight_total.astype(jnp.bfloat16))
```

```python
import jax
import jax.numpy as jnp
from jax import lax
from jax.experimental import pallas as pl
from jax.experimental.pallas import tpu as pltpu
from jax.sharding import PartitionSpec as P

CAP = 2
N_Y = 4
LABEL_ROWS = 16
VMEM_BYTES = 56 * 1024 * 1024


def along_col(dy, dc):
    return [
        (y * 2 + c, ((y + dy) % N_Y) * 2 + (c + dc) % 2) for y in range(N_Y) for c in range(2)
    ]


def send_y(values, dy):
    return lax.ppermute(values, "col", along_col(dy, 0))


def swap_core(values):
    return lax.ppermute(values, "col", along_col(0, 1))


def pack_kernel(packing, blocks, outgoing, source, label, count):
    owners = outgoing.shape[0]
    block_count, block_rows = blocks.shape[0], blocks.shape[1]
    for owner in range(owners):
        count[owner] = 0
    for slot in range(owners * CAP):
        source[slot] = 0
        label[slot] = -1

    def route(block, carry):
        target = packing[block]
        owner = target // block_count
        rank = count[owner]
        count[owner] = rank + 1
        source[owner * CAP + rank] = block
        label[owner * CAP + rank] = target - owner * block_count
        return carry

    lax.fori_loop(0, block_count, route, 0)

    def fill(owner, carry):
        for rank in range(CAP):
            slot = owner * CAP + rank
            outgoing[owner, rank * block_rows : (rank + 1) * block_rows, :] = blocks[source[slot]]
            mark = jnp.full((LABEL_ROWS, 128), label[slot], jnp.int32).astype(jnp.float32)
            outgoing[owner, CAP * block_rows :, rank * 128 : (rank + 1) * 128] = mark.astype(
                jnp.bfloat16
            )
        outgoing[owner, CAP * block_rows :, CAP * 128 :] = jnp.zeros(
            (LABEL_ROWS, blocks.shape[2] - CAP * 128), jnp.bfloat16
        )
        return carry

    lax.fori_loop(0, owners, fill, 0)


def pack_blocks(packing, blocks, owners):
    block_count, block_rows, cols = blocks.shape
    return pl.pallas_call(
        pack_kernel,
        out_shape=jax.ShapeDtypeStruct((owners, CAP * block_rows + LABEL_ROWS, cols), blocks.dtype),
        in_specs=[
            pl.BlockSpec(memory_space=pltpu.SMEM),
            pl.BlockSpec(memory_space=pltpu.VMEM),
        ],
        out_specs=pl.BlockSpec(memory_space=pltpu.VMEM),
        scratch_shapes=[
            pltpu.SMEM((owners * CAP,), jnp.int32),
            pltpu.SMEM((owners * CAP,), jnp.int32),
            pltpu.SMEM((owners,), jnp.int32),
        ],
        compiler_params=pltpu.CompilerParams(vmem_limit_bytes=VMEM_BYTES),
    )(packing, blocks)


def place_kernel(where, arrived, rows):
    block_rows = rows.shape[1]

    def place(slot, carry):
        spot = where[slot]
        start = pl.multiple_of((spot % CAP) * block_rows, block_rows)
        rows[slot] = arrived[spot // CAP, pl.ds(start, block_rows), :]
        return carry

    lax.fori_loop(0, rows.shape[0], place, 0)


def place_blocks(arrived, block_count, block_rows):
    owners, _, cols = arrived.shape
    label = arrived[:, CAP * block_rows, : CAP * 128].reshape(owners, CAP, 128)[:, :, 0]
    label = label.astype(jnp.int32).reshape(owners * CAP)
    spots = jnp.arange(owners * CAP, dtype=jnp.int32)
    hit = jnp.arange(block_count, dtype=jnp.int32)[:, None] == label[None, :]
    where = jnp.sum(jnp.where(hit, spots[None, :], 0), axis=1)
    return pl.pallas_call(
        place_kernel,
        out_shape=jax.ShapeDtypeStruct((block_count, block_rows, cols), arrived.dtype),
        in_specs=[
            pl.BlockSpec(memory_space=pltpu.SMEM),
            pl.BlockSpec(memory_space=pltpu.VMEM),
        ],
        out_specs=pl.BlockSpec(memory_space=pltpu.VMEM),
        compiler_params=pltpu.CompilerParams(vmem_limit_bytes=VMEM_BYTES),
    )(where, arrived)


def dot(left, right, left_dim, right_dim):
    return lax.dot_general(
        left, right, (((left_dim,), (right_dim,)), ((), ())), preferred_element_type=jnp.float32
    )


def normalize(values):
    centred = values - jnp.mean(values, axis=-1, keepdims=True)
    inv_std = lax.rsqrt(jnp.mean(centred * centred, axis=-1, keepdims=True) + 1e-06)
    return (centred * inv_std, inv_std)


def norm_grad(upstream, normed, inv_std, gain):
    scaled = upstream * gain
    mean_one = jnp.mean(scaled, axis=-1, keepdims=True)
    mean_two = jnp.mean(scaled * normed, axis=-1, keepdims=True)
    return (scaled - mean_one - normed * mean_two) * inv_std


def heads_kernel(
    order, own, other, weight, gain_q, gain_k, seg_col, seg_row, upstream,
    out, grad, grad_weight, total,
):
    size = gain_q.shape[-1]
    depth = own.shape[2]
    blocks = own.shape[0]

    def spot(index):
        return pl.ds(pl.multiple_of(order[index] * depth, depth), depth)

    total[...] = jnp.zeros_like(total)

    def project(block, carry):
        total[...] += dot(own[block], weight[spot(block), :], 1, 0)
        total[...] += dot(other[block], weight[spot(blocks + block), :], 1, 0)
        return carry

    lax.fori_loop(0, blocks, project, 0)
    projected = total[...]
    query_hat, query_inv = normalize(projected[:, :size])
    key_hat, key_inv = normalize(projected[:, size : 2 * size])
    gain_query, gain_key = gain_q[0], gain_k[0]
    query = (query_hat * gain_query).astype(jnp.bfloat16)
    key = (key_hat * gain_key).astype(jnp.bfloat16)
    value = projected[:, 2 * size :].astype(jnp.bfloat16)
    factor = 1.0 / size**0.5
    weights = jnp.exp(dot(query, key, 1, 1) * factor)
    weights = jnp.where(seg_col[...] == seg_row[...], weights, 0.0)
    probs = weights * (1.0 / jnp.sum(weights, axis=-1, keepdims=True))
    probs_half = probs.astype(jnp.bfloat16)
    up = upstream[...]
    out[...] = dot(probs_half, value, 1, 0).astype(jnp.bfloat16)
    grad[:, 2 * size :] = dot(probs_half, up, 0, 0).astype(jnp.bfloat16)
    grad_probs = dot(up, value, 1, 1)
    inner = jnp.sum(probs * grad_probs, axis=-1, keepdims=True)
    grad_scores = (probs * (grad_probs - inner) * factor).astype(jnp.bfloat16)
    grad_qn = dot(grad_scores, key, 1, 0)
    grad_kn = dot(grad_scores, query, 0, 0)
    grad[:, :size] = norm_grad(grad_qn, query_hat, query_inv, gain_query).astype(jnp.bfloat16)
    grad[:, size : 2 * size] = norm_grad(grad_kn, key_hat, key_inv, gain_key).astype(jnp.bfloat16)

    def weigh(block, carry):
        grad_weight[spot(block), :] = dot(own[block], grad[...], 0, 0).astype(jnp.bfloat16)
        grad_weight[spot(blocks + block), :] = dot(other[block], grad[...], 0, 0).astype(
            jnp.bfloat16
        )
        return carry

    lax.fori_loop(0, blocks, weigh, 0)


def run_heads(order, own, other, weight, gain_query, gain_key, segments, upstream):
    heads, size = gain_query.shape
    rows = segments.shape[0]
    depth = weight.shape[0]
    width = 3 * size
    whole = lambda head, order: (0, 0, 0)
    per_head = lambda head, order: (0, head)
    one = lambda head, order: (head, 0, 0)
    fixed = lambda head, order: (0, 0)
    return pl.pallas_call(
        heads_kernel,
        out_shape=(
            jax.ShapeDtypeStruct((rows, heads * size), jnp.bfloat16),
            jax.ShapeDtypeStruct((rows, heads * width), jnp.bfloat16),
            jax.ShapeDtypeStruct((depth, heads * width), jnp.bfloat16),
        ),
        grid_spec=pltpu.PrefetchScalarGridSpec(
            num_scalar_prefetch=1,
            grid=(heads,),
            in_specs=[
                pl.BlockSpec(own.shape, whole),
                pl.BlockSpec(other.shape, whole),
                pl.BlockSpec((depth, width), per_head),
                pl.BlockSpec((1, 1, size), one),
                pl.BlockSpec((1, 1, size), one),
                pl.BlockSpec((rows, 1), fixed),
                pl.BlockSpec((1, rows), fixed),
                pl.BlockSpec((rows, size), per_head),
            ],
            out_specs=(
                pl.BlockSpec((rows, size), per_head),
                pl.BlockSpec((rows, width), per_head),
                pl.BlockSpec((depth, width), per_head),
            ),
            scratch_shapes=[pltpu.VMEM((rows, width), jnp.float32)],
        ),
        compiler_params=pltpu.CompilerParams(vmem_limit_bytes=VMEM_BYTES),
        cost_estimate=pl.CostEstimate(
            flops=4 * rows * depth * heads * width,
            bytes_accessed=4 * depth * heads * width + 2 * rows * depth,
            transcendentals=heads * rows * rows,
        ),
    )(
        order, own, other, weight, gain_query[:, None, :], gain_key[:, None, :],
        segments[:, None], segments[None, :], upstream,
    )


def terms_kernel(order, grad, weight, terms):
    terms[0] = dot(grad[...], weight[...], 1, 1).astype(jnp.bfloat16)


def row_terms(order, grad, weight):
    rows, cols = grad.shape
    blocks = order.shape[0]
    depth = weight.shape[0] // (2 * N_Y)
    return pl.pallas_call(
        terms_kernel,
        out_shape=jax.ShapeDtypeStruct((blocks, rows, depth), jnp.bfloat16),
        grid_spec=pltpu.PrefetchScalarGridSpec(
            num_scalar_prefetch=1,
            grid=(blocks,),
            in_specs=[
                pl.BlockSpec((rows, cols), lambda block, order: (0, 0)),
                pl.BlockSpec((depth, cols), lambda block, order: (order[block], 0)),
            ],
            out_specs=pl.BlockSpec((1, rows, depth), lambda block, order: (block, 0, 0)),
        ),
        compiler_params=pltpu.CompilerParams(vmem_limit_bytes=VMEM_BYTES),
        cost_estimate=pl.CostEstimate(
            flops=2 * rows * depth * blocks * cols,
            bytes_accessed=2 * (rows * cols + blocks * depth * (cols + rows)),
            transcendentals=0,
        ),
    )(order, grad, weight)


def total_of(*terms):
    return sum(term.astype(jnp.float32) for term in terms).astype(jnp.bfloat16)


def gather_rows(own_rows):
    half = own_rows.shape[0] // 2
    below, above = send_y(own_rows, 1), send_y(own_rows, -1)
    far = jnp.concatenate([send_y(below[:half], 1), send_y(above[half:], -1)], axis=0)
    own = jnp.stack([own_rows, below, above, far])
    return own, swap_core(own)


def scatter_rows(own, other):
    here, after, before, far = [
        total_of(own[i], arrived) for i, arrived in enumerate(swap_core(other))
    ]
    half = here.shape[0] // 2
    up, down = send_y(far[:half], 1), send_y(far[half:], -1)
    after = jnp.concatenate([total_of(after[:half], up), after[half:]], axis=0)
    before = jnp.concatenate([before[:half], total_of(before[half:], down)], axis=0)
    return total_of(here, send_y(after, 1), send_y(before, -1))


def shards(loader_rows, packing, segment_ids, qkv_weight, gain_query, gain_key, out_grad):
    owners = lax.axis_size("row")
    block_count, block_rows, feature_cols = loader_rows.shape
    weight_panel = lax.all_gather(qkv_weight, "row", axis=0, tiled=True)

    outgoing = pack_blocks(packing, loader_rows, owners)
    arrived = lax.all_to_all(outgoing, "row", split_axis=0, concat_axis=0, tiled=True)
    own_rows = place_blocks(arrived, block_count, block_rows)
    own_rows = own_rows.reshape(block_count * block_rows, feature_cols)
    own, other = gather_rows(own_rows)

    col = lax.axis_index("col")
    y, core = col // 2, col % 2
    offsets = jnp.array([0, -1, 1, 2], jnp.int32)
    ys = (y + offsets) % N_Y
    order = jnp.concatenate([ys * 2 + core, ys * 2 + 1 - core]).astype(jnp.int32)
    attn_out, grad_flat, grad_panel = run_heads(
        order, own, other, weight_panel, gain_query, gain_key, segment_ids[0], out_grad
    )
    grad_weight = lax.psum_scatter(grad_panel, "row", scatter_dimension=0, tiled=True)

    ys = (y - offsets) % N_Y
    terms_other = row_terms((ys * 2 + 1 - core).astype(jnp.int32), grad_flat, weight_panel)
    terms_own = row_terms((ys * 2 + core).astype(jnp.int32), grad_flat, weight_panel)
    grad_rows = scatter_rows(terms_own, terms_other)
    return (attn_out, grad_rows, grad_weight)


def solution(mesh):
    in_specs = (
        P("row", None, "col"),
        P("row"),
        P("row", None),
        P("row", "col"),
        P("col", None),
        P("col", None),
        P("row", "col"),
    )
    out_specs = (P("row", "col"), P("row", "col"), P("row", "col"))
    return jax.shard_map(shards, mesh=mesh, in_specs=in_specs, out_specs=out_specs, check_vma=False)
```

```python
import jax
import jax.numpy as jnp
from jax import lax
from jax.experimental import pallas as pl
from jax.experimental.pallas import tpu as pltpu
from jax.sharding import PartitionSpec as P

CAP = 2
N_Y = 4
LABEL_COLS = 128
VMEM_BYTES = 56 * 1024 * 1024


def along_col(dy, dc):
    return [
        (y * 2 + c, ((y + dy) % N_Y) * 2 + (c + dc) % 2) for y in range(N_Y) for c in range(2)
    ]


def send_y(values, dy):
    return lax.ppermute(values, "col", along_col(dy, 0))


def swap_core(values):
    return lax.ppermute(values, "col", along_col(0, 1))


def pack_kernel(packing, blocks, outgoing, source, label, count):
    owners = outgoing.shape[0]
    block_count, block_rows, cols = blocks.shape
    label_rows = block_rows // CAP
    for owner in range(owners):
        count[owner] = 0
    for slot in range(owners * CAP):
        source[slot] = 0
        label[slot] = -1

    def route(block, carry):
        target = packing[block]
        owner = target // block_count
        rank = count[owner]
        count[owner] = rank + 1
        source[owner * CAP + rank] = block
        label[owner * CAP + rank] = target - owner * block_count
        return carry

    lax.fori_loop(0, block_count, route, 0)

    def fill(owner, carry):
        for rank in range(CAP):
            slot = owner * CAP + rank
            outgoing[owner, :, rank * cols : (rank + 1) * cols] = blocks[source[slot]]
            mark = jnp.full((label_rows, LABEL_COLS), label[slot], jnp.int32).astype(jnp.float32)
            outgoing[owner, rank * label_rows : (rank + 1) * label_rows, CAP * cols :] = mark.astype(
                jnp.bfloat16
            )
        return carry

    lax.fori_loop(0, owners, fill, 0)


def pack_blocks(packing, blocks, owners):
    block_count, block_rows, cols = blocks.shape
    return pl.pallas_call(
        pack_kernel,
        out_shape=jax.ShapeDtypeStruct((owners, block_rows, CAP * cols + LABEL_COLS), blocks.dtype),
        in_specs=[
            pl.BlockSpec(memory_space=pltpu.SMEM),
            pl.BlockSpec(memory_space=pltpu.VMEM),
        ],
        out_specs=pl.BlockSpec(memory_space=pltpu.VMEM),
        scratch_shapes=[
            pltpu.SMEM((owners * CAP,), jnp.int32),
            pltpu.SMEM((owners * CAP,), jnp.int32),
            pltpu.SMEM((owners,), jnp.int32),
        ],
        compiler_params=pltpu.CompilerParams(vmem_limit_bytes=VMEM_BYTES),
    )(packing, blocks)


def place_kernel(where, arrived, rows):
    cols = rows.shape[2]

    def place(slot, carry):
        spot = where[slot]
        start = pl.multiple_of((spot % CAP) * cols, cols)
        rows[slot] = arrived[spot // CAP, :, pl.ds(start, cols)]
        return carry

    lax.fori_loop(0, rows.shape[0], place, 0)


def place_blocks(arrived, block_count):
    owners, block_rows, cols = arrived.shape
    cols = (cols - LABEL_COLS) // CAP
    label = arrived[:, :: block_rows // CAP, CAP * cols]
    label = label.astype(jnp.int32).reshape(owners * CAP)
    spots = jnp.arange(owners * CAP, dtype=jnp.int32)
    hit = jnp.arange(block_count, dtype=jnp.int32)[:, None] == label[None, :]
    where = jnp.sum(jnp.where(hit, spots[None, :], 0), axis=1)
    return pl.pallas_call(
        place_kernel,
        out_shape=jax.ShapeDtypeStruct((block_count, block_rows, cols), arrived.dtype),
        in_specs=[
            pl.BlockSpec(memory_space=pltpu.SMEM),
            pl.BlockSpec(memory_space=pltpu.VMEM),
        ],
        out_specs=pl.BlockSpec(memory_space=pltpu.VMEM),
        compiler_params=pltpu.CompilerParams(vmem_limit_bytes=VMEM_BYTES),
    )(where, arrived)


def dot(left, right, left_dim, right_dim):
    return lax.dot_general(
        left, right, (((left_dim,), (right_dim,)), ((), ())), preferred_element_type=jnp.float32
    )


def normalize(values):
    centred = values - jnp.mean(values, axis=-1, keepdims=True)
    inv_std = lax.rsqrt(jnp.mean(centred * centred, axis=-1, keepdims=True) + 1e-06)
    return (centred * inv_std, inv_std)


def norm_grad(upstream, normed, inv_std, gain):
    scaled = upstream * gain
    mean_one = jnp.mean(scaled, axis=-1, keepdims=True)
    mean_two = jnp.mean(scaled * normed, axis=-1, keepdims=True)
    return (scaled - mean_one - normed * mean_two) * inv_std


def attend(projected, gain_query, gain_key, seg_col, seg_row, up):
    size = up.shape[1]
    query_hat, query_inv = normalize(projected[:, :size])
    key_hat, key_inv = normalize(projected[:, size : 2 * size])
    query = (query_hat * gain_query).astype(jnp.bfloat16)
    key = (key_hat * gain_key).astype(jnp.bfloat16)
    value = projected[:, 2 * size :].astype(jnp.bfloat16)
    factor = 1.0 / size**0.5
    weights = jnp.exp(dot(query, key, 1, 1) * factor)
    weights = jnp.where(seg_col == seg_row, weights, 0.0)
    probs = weights * (1.0 / jnp.sum(weights, axis=-1, keepdims=True))
    probs_half = probs.astype(jnp.bfloat16)
    out = dot(probs_half, value, 1, 0).astype(jnp.bfloat16)
    grad_value = dot(probs_half, up, 0, 0)
    grad_probs = dot(up, value, 1, 1)
    inner = jnp.sum(probs * grad_probs, axis=-1, keepdims=True)
    grad_scores = (probs * (grad_probs - inner) * factor).astype(jnp.bfloat16)
    grad_query = norm_grad(dot(grad_scores, key, 1, 0), query_hat, query_inv, gain_query)
    grad_key = norm_grad(dot(grad_scores, query, 0, 0), key_hat, key_inv, gain_key)
    grads = (grad_query, grad_key, grad_value)
    return out, [part.astype(jnp.bfloat16) for part in grads]


def heads_kernel(
    order, own, other, weight, gain_q, gain_k, seg_col, seg_row, upstream,
    out, grad, grad_weight, kept, total,
):
    size = gain_q.shape[-1]
    heads = gain_q.shape[0]
    blocks = kept.shape[0]
    step = pl.program_id(0)

    def project(rows):
        kept[step] = rows[0]
        total[...] += dot(rows[0], weight[...], 1, 0)

    @pl.when(step == 0)
    def _():
        total[...] = jnp.zeros_like(total)

    @pl.when(step < blocks // 2)
    def _():
        project(own)

    @pl.when((step >= blocks // 2) & (step < blocks))
    def _():
        project(other)

    @pl.when(step == blocks - 1)
    def _():
        for head in range(heads):
            left = 3 * head * size
            result, parts = attend(
                total[:, left : left + 3 * size], gain_q[head], gain_k[head],
                seg_col[...], seg_row[...], upstream[:, head * size : (head + 1) * size],
            )
            out[:, head * size : (head + 1) * size] = result
            for kind, part in enumerate(parts):
                grad[:, left + kind * size : left + (kind + 1) * size] = part

    @pl.when(step >= blocks)
    def _():
        grad_weight[...] = dot(kept[step - blocks], grad[...], 0, 0).astype(jnp.bfloat16)


def run_heads(order, own, other, weight, gain_query, gain_key, segments, upstream):
    heads, size = gain_query.shape
    rows = segments.shape[0]
    depth, cols = weight.shape
    blocks = order.shape[0]
    half = blocks // 2
    width = depth // blocks
    fixed = lambda step, order: (0, 0)
    cube = lambda step, order: (0, 0, 0)
    return pl.pallas_call(
        heads_kernel,
        out_shape=(
            jax.ShapeDtypeStruct((rows, heads * size), jnp.bfloat16),
            jax.ShapeDtypeStruct((rows, cols), jnp.bfloat16),
            jax.ShapeDtypeStruct((depth, cols), jnp.bfloat16),
        ),
        grid_spec=pltpu.PrefetchScalarGridSpec(
            num_scalar_prefetch=1,
            grid=(2 * blocks,),
            in_specs=[
                pl.BlockSpec(
                    (1, rows, width), lambda step, order: (jnp.minimum(step, half - 1), 0, 0)
                ),
                pl.BlockSpec(
                    (1, rows, width), lambda step, order: (jnp.clip(step - half, 0, half - 1), 0, 0)
                ),
                pl.BlockSpec(
                    (width, cols), lambda step, order: (order[jnp.minimum(step, blocks - 1)], 0)
                ),
                pl.BlockSpec((heads, 1, size), cube),
                pl.BlockSpec((heads, 1, size), cube),
                pl.BlockSpec((rows, 1), fixed),
                pl.BlockSpec((1, rows), fixed),
                pl.BlockSpec((rows, heads * size), fixed),
            ],
            out_specs=(
                pl.BlockSpec((rows, heads * size), fixed),
                pl.BlockSpec((rows, cols), fixed),
                pl.BlockSpec(
                    (width, cols), lambda step, order: (order[jnp.maximum(step - blocks, 0)], 0)
                ),
            ),
            scratch_shapes=[
                pltpu.VMEM((blocks, rows, width), jnp.bfloat16),
                pltpu.VMEM((rows, cols), jnp.float32),
            ],
        ),
        compiler_params=pltpu.CompilerParams(vmem_limit_bytes=VMEM_BYTES),
        cost_estimate=pl.CostEstimate(
            flops=4 * rows * depth * cols,
            bytes_accessed=4 * depth * cols + 2 * rows * depth,
            transcendentals=heads * rows * rows,
        ),
    )(
        order, own, other, weight, gain_query[:, None, :], gain_key[:, None, :],
        segments[:, None], segments[None, :], upstream,
    )


def terms_kernel(order, grad, weight, terms):
    terms[0] = dot(grad[...], weight[...], 1, 1).astype(jnp.bfloat16)


def row_terms(order, grad, weight):
    rows, cols = grad.shape
    blocks = order.shape[0]
    depth = weight.shape[0] // (2 * N_Y)
    return pl.pallas_call(
        terms_kernel,
        out_shape=jax.ShapeDtypeStruct((blocks, rows, depth), jnp.bfloat16),
        grid_spec=pltpu.PrefetchScalarGridSpec(
            num_scalar_prefetch=1,
            grid=(blocks,),
            in_specs=[
                pl.BlockSpec((rows, cols), lambda block, order: (0, 0)),
                pl.BlockSpec((depth, cols), lambda block, order: (order[block], 0)),
            ],
            out_specs=pl.BlockSpec((1, rows, depth), lambda block, order: (block, 0, 0)),
        ),
        compiler_params=pltpu.CompilerParams(vmem_limit_bytes=VMEM_BYTES),
        cost_estimate=pl.CostEstimate(
            flops=2 * rows * depth * blocks * cols,
            bytes_accessed=2 * (rows * cols + blocks * depth * (cols + rows)),
            transcendentals=0,
        ),
    )(order, grad, weight)


def total_of(*terms):
    return sum(term.astype(jnp.float32) for term in terms).astype(jnp.bfloat16)


def gather_rows(own_rows):
    half = own_rows.shape[0] // 2
    below, above = send_y(own_rows, 1), send_y(own_rows, -1)
    far = jnp.concatenate([send_y(below[:half], 1), send_y(above[half:], -1)], axis=0)
    own = jnp.stack([own_rows, below, above, far])
    return own, swap_core(own)


def scatter_rows(own, other):
    here, after, before, far = [
        total_of(own[i], arrived) for i, arrived in enumerate(swap_core(other))
    ]
    half = here.shape[0] // 2
    up, down = send_y(far[:half], 1), send_y(far[half:], -1)
    after = jnp.concatenate([total_of(after[:half], up), after[half:]], axis=0)
    before = jnp.concatenate([before[:half], total_of(before[half:], down)], axis=0)
    return total_of(here, send_y(after, 1), send_y(before, -1))


def shards(loader_rows, packing, segment_ids, qkv_weight, gain_query, gain_key, out_grad):
    owners = lax.axis_size("row")
    block_count, block_rows, feature_cols = loader_rows.shape
    weight_panel = lax.all_gather(qkv_weight, "row", axis=0, tiled=True)

    outgoing = pack_blocks(packing, loader_rows, owners)
    arrived = lax.all_to_all(outgoing, "row", split_axis=0, concat_axis=0, tiled=True)
    own_rows = place_blocks(arrived, block_count)
    own_rows = own_rows.reshape(block_count * block_rows, feature_cols)
    own, other = gather_rows(own_rows)

    col = lax.axis_index("col")
    y, core = col // 2, col % 2
    offsets = jnp.array([0, -1, 1, 2], jnp.int32)
    ys = (y + offsets) % N_Y
    order = jnp.concatenate([ys * 2 + core, ys * 2 + 1 - core]).astype(jnp.int32)
    attn_out, grad_flat, grad_panel = run_heads(
        order, own, other, weight_panel, gain_query, gain_key, segment_ids[0], out_grad
    )
    grad_weight = lax.psum_scatter(grad_panel, "row", scatter_dimension=0, tiled=True)

    ys = (y - offsets) % N_Y
    terms_other = row_terms((ys * 2 + 1 - core).astype(jnp.int32), grad_flat, weight_panel)
    terms_own = row_terms((ys * 2 + core).astype(jnp.int32), grad_flat, weight_panel)
    grad_rows = scatter_rows(terms_own, terms_other)
    return (attn_out, grad_rows, grad_weight)


def solution(mesh):
    in_specs = (
        P("row", None, "col"),
        P("row"),
        P("row", None),
        P("row", "col"),
        P("col", None),
        P("col", None),
        P("row", "col"),
    )
    out_specs = (P("row", "col"), P("row", "col"), P("row", "col"))
    return jax.shard_map(shards, mesh=mesh, in_specs=in_specs, out_specs=out_specs, check_vma=False)
```

```python
import jax
import jax.numpy as jnp
from jax import lax
from jax.experimental import pallas as pl
from jax.experimental.pallas import tpu as pltpu
from jax.sharding import PartitionSpec as P

CAP = 2
N_RING = 4
LABEL_COLS = 128
VMEM_BYTES = 56 * 1024 * 1024


def along_col(dy, dc):
    return [
        (y * 2 + c, ((y + dy) % N_RING) * 2 + (c + dc) % 2) for y in range(N_RING) for c in range(2)
    ]


def along_row(dx, dz):
    return [
        (x * N_RING + z, ((x + dx) % N_RING) * N_RING + (z + dz) % N_RING)
        for x in range(N_RING)
        for z in range(N_RING)
    ]


def send_x(values, step):
    return lax.ppermute(values, "row", along_row(step, 0))


def send_z(values, step):
    return lax.ppermute(values, "row", along_row(0, step))


def send_y(values, step):
    return lax.ppermute(values, "col", along_col(step, 0))


def send_to_half(values, step):
    pairs = []
    for place in range(N_RING * N_RING):
        x, z = divmod(place, N_RING)
        to = (z + step) % N_RING
        for y in range(N_RING):
            col = 2 * y + to // 2
            pairs.append((place * 2 * N_RING + col, (x * N_RING + to) * 2 * N_RING + col))
    return lax.ppermute(values, ("row", "col"), pairs)


def swap_core(values):
    return lax.ppermute(values, "col", along_col(0, 1))


def pack_kernel(packing, blocks, outgoing, source, label, count):
    owners = outgoing.shape[0]
    block_count, block_rows, cols = blocks.shape
    label_rows = block_rows // CAP
    for owner in range(owners):
        count[owner] = 0
    for slot in range(owners * CAP):
        source[slot] = 0
        label[slot] = -1

    def route(block, carry):
        target = packing[block]
        owner = target // block_count
        rank = count[owner]
        count[owner] = rank + 1
        source[owner * CAP + rank] = block
        label[owner * CAP + rank] = target - owner * block_count
        return carry

    lax.fori_loop(0, block_count, route, 0)

    def fill(owner, carry):
        for rank in range(CAP):
            slot = owner * CAP + rank
            outgoing[owner, :, rank * cols : (rank + 1) * cols] = blocks[source[slot]]
            mark = jnp.full((label_rows, LABEL_COLS), label[slot], jnp.int32).astype(jnp.float32)
            outgoing[owner, rank * label_rows : (rank + 1) * label_rows, CAP * cols :] = mark.astype(
                jnp.bfloat16
            )
        return carry

    lax.fori_loop(0, owners, fill, 0)


def pack_blocks(packing, blocks, owners):
    block_count, block_rows, cols = blocks.shape
    return pl.pallas_call(
        pack_kernel,
        out_shape=jax.ShapeDtypeStruct((owners, block_rows, CAP * cols + LABEL_COLS), blocks.dtype),
        in_specs=[
            pl.BlockSpec(memory_space=pltpu.SMEM),
            pl.BlockSpec(memory_space=pltpu.VMEM),
        ],
        out_specs=pl.BlockSpec(memory_space=pltpu.VMEM),
        scratch_shapes=[
            pltpu.SMEM((owners * CAP,), jnp.int32),
            pltpu.SMEM((owners * CAP,), jnp.int32),
            pltpu.SMEM((owners,), jnp.int32),
        ],
        compiler_params=pltpu.CompilerParams(vmem_limit_bytes=VMEM_BYTES),
    )(packing, blocks)


def place_kernel(where, arrived, rows):
    cols = rows.shape[2]

    def place(slot, carry):
        spot = where[slot]
        start = pl.multiple_of((spot % CAP) * cols, cols)
        rows[slot] = arrived[spot // CAP, :, pl.ds(start, cols)]
        return carry

    lax.fori_loop(0, rows.shape[0], place, 0)


def place_blocks(arrived, block_count):
    owners, block_rows, cols = arrived.shape
    cols = (cols - LABEL_COLS) // CAP
    label = arrived[:, :: block_rows // CAP, CAP * cols]
    label = label.astype(jnp.int32).reshape(owners * CAP)
    spots = jnp.arange(owners * CAP, dtype=jnp.int32)
    hit = jnp.arange(block_count, dtype=jnp.int32)[:, None] == label[None, :]
    where = jnp.sum(jnp.where(hit, spots[None, :], 0), axis=1)
    return pl.pallas_call(
        place_kernel,
        out_shape=jax.ShapeDtypeStruct((block_count, block_rows, cols), arrived.dtype),
        in_specs=[
            pl.BlockSpec(memory_space=pltpu.SMEM),
            pl.BlockSpec(memory_space=pltpu.VMEM),
        ],
        out_specs=pl.BlockSpec(memory_space=pltpu.VMEM),
        compiler_params=pltpu.CompilerParams(vmem_limit_bytes=VMEM_BYTES),
    )(where, arrived)


def dot(left, right, left_dim, right_dim):
    return lax.dot_general(
        left, right, (((left_dim,), (right_dim,)), ((), ())), preferred_element_type=jnp.float32
    )


def normalize(values):
    centred = values - jnp.mean(values, axis=-1, keepdims=True)
    inv_std = lax.rsqrt(jnp.mean(centred * centred, axis=-1, keepdims=True) + 1e-06)
    return (centred * inv_std, inv_std)


def norm_grad(upstream, normed, inv_std, gain):
    scaled = upstream * gain
    mean_one = jnp.mean(scaled, axis=-1, keepdims=True)
    mean_two = jnp.mean(scaled * normed, axis=-1, keepdims=True)
    return (scaled - mean_one - normed * mean_two) * inv_std


def attend(projected, gain_query, gain_key, seg_col, seg_row, up):
    size = up.shape[1]
    query_hat, query_inv = normalize(projected[:, :size])
    key_hat, key_inv = normalize(projected[:, size : 2 * size])
    query = (query_hat * gain_query).astype(jnp.bfloat16)
    key = (key_hat * gain_key).astype(jnp.bfloat16)
    value = projected[:, 2 * size :].astype(jnp.bfloat16)
    factor = 1.0 / size**0.5
    weights = jnp.exp(dot(query, key, 1, 1) * factor)
    weights = jnp.where(seg_col == seg_row, weights, 0.0)
    probs = weights * (1.0 / jnp.sum(weights, axis=-1, keepdims=True))
    probs_half = probs.astype(jnp.bfloat16)
    out = dot(probs_half, value, 1, 0).astype(jnp.bfloat16)
    grad_value = dot(probs_half, up, 0, 0)
    grad_probs = dot(up, value, 1, 1)
    inner = jnp.sum(probs * grad_probs, axis=-1, keepdims=True)
    grad_scores = (probs * (grad_probs - inner) * factor).astype(jnp.bfloat16)
    grad_query = norm_grad(dot(grad_scores, key, 1, 0), query_hat, query_inv, gain_query)
    grad_key = norm_grad(dot(grad_scores, query, 0, 0), key_hat, key_inv, gain_key)
    grads = (grad_query, grad_key, grad_value)
    return out, [part.astype(jnp.bfloat16) for part in grads]


def heads_kernel(
    order, own, other, weight, gain_q, gain_k, seg_col, seg_row, upstream, out, top, bottom, total
):
    size = gain_q.shape[-1]
    heads = gain_q.shape[0]
    half = top.shape[0]
    step, blocks = pl.program_id(0), pl.num_programs(0)

    @pl.when(step == 0)
    def _():
        total[...] = jnp.zeros_like(total)

    @pl.when(step < blocks // 2)
    def _():
        total[...] += dot(own[0], weight[...], 1, 0)

    @pl.when(step >= blocks // 2)
    def _():
        total[...] += dot(other[0], weight[...], 1, 0)

    @pl.when(step == blocks - 1)
    def _():
        for head in range(heads):
            left = 3 * head * size
            result, parts = attend(
                total[:, left : left + 3 * size], gain_q[head], gain_k[head],
                seg_col[...], seg_row[...], upstream[:, head * size : (head + 1) * size],
            )
            out[:, head * size : (head + 1) * size] = result
            for kind, part in enumerate(parts):
                span = slice(left + kind * size, left + (kind + 1) * size)
                top[:, span], bottom[:, span] = part[:half], part[half:]


def run_heads(order, own, other, weight, gain_query, gain_key, segments, upstream):
    heads, size = gain_query.shape
    rows = segments.shape[0]
    depth, cols = weight.shape
    blocks = order.shape[0]
    half = blocks // 2
    width = depth // blocks
    fixed = lambda step, order: (0, 0)
    cube = lambda step, order: (0, 0, 0)
    return pl.pallas_call(
        heads_kernel,
        out_shape=(
            jax.ShapeDtypeStruct((rows, heads * size), jnp.bfloat16),
            jax.ShapeDtypeStruct((rows // 2, cols), jnp.bfloat16),
            jax.ShapeDtypeStruct((rows // 2, cols), jnp.bfloat16),
        ),
        grid_spec=pltpu.PrefetchScalarGridSpec(
            num_scalar_prefetch=1,
            grid=(blocks,),
            in_specs=[
                pl.BlockSpec(
                    (1, rows, width), lambda step, order: (jnp.minimum(step, half - 1), 0, 0)
                ),
                pl.BlockSpec(
                    (1, rows, width), lambda step, order: (jnp.maximum(step - half, 0), 0, 0)
                ),
                pl.BlockSpec((width, cols), lambda step, order: (order[step], 0)),
                pl.BlockSpec((heads, 1, size), cube),
                pl.BlockSpec((heads, 1, size), cube),
                pl.BlockSpec((rows, 1), fixed),
                pl.BlockSpec((1, rows), fixed),
                pl.BlockSpec((rows, heads * size), fixed),
            ],
            out_specs=(
                pl.BlockSpec((rows, heads * size), fixed),
                pl.BlockSpec((rows // 2, cols), fixed),
                pl.BlockSpec((rows // 2, cols), fixed),
            ),
            scratch_shapes=[pltpu.VMEM((rows, cols), jnp.float32)],
        ),
        compiler_params=pltpu.CompilerParams(vmem_limit_bytes=VMEM_BYTES),
        cost_estimate=pl.CostEstimate(
            flops=2 * rows * depth * cols,
            bytes_accessed=2 * depth * cols + 2 * rows * depth,
            transcendentals=heads * rows * rows,
        ),
    )(
        order, own, other, weight, gain_query[:, None, :], gain_key[:, None, :],
        segments[:, None], segments[None, :], upstream,
    )


def weigh_near_kernel(table, low, high, *refs):
    grads, terms = refs[:-1], refs[-1]
    half = grads[0].shape[0]
    total = 0.0
    for sequence, rows in enumerate((low[0, 0], low[0, 1], high[0, 0])):
        top, bottom = grads[2 * sequence : 2 * sequence + 2]
        total += dot(rows[:half], top[...], 0, 0) + dot(rows[half:], bottom[...], 0, 0)
    terms[0] = total


def weigh_near(table, shared, grads):
    _, count, length, width = shared.shape
    pieces, cols = table.shape[0], grads[0].shape[1]
    return pl.pallas_call(
        weigh_near_kernel,
        out_shape=jax.ShapeDtypeStruct((pieces, width, cols), jnp.float32),
        grid_spec=pltpu.PrefetchScalarGridSpec(
            num_scalar_prefetch=1,
            grid=(pieces,),
            in_specs=[
                pl.BlockSpec(
                    (1, count, length, width), lambda piece, table: (2 * table[piece], 0, 0, 0)
                ),
                pl.BlockSpec(
                    (1, 1, length, width), lambda piece, table: (2 * table[piece] + 1, 0, 0, 0)
                ),
            ]
            + [pl.BlockSpec(grad.shape, lambda piece, table: (0, 0)) for grad in grads],
            out_specs=pl.BlockSpec((1, width, cols), lambda piece, table: (piece, 0, 0)),
        ),
        compiler_params=pltpu.CompilerParams(vmem_limit_bytes=VMEM_BYTES),
        cost_estimate=pl.CostEstimate(
            flops=6 * pieces * length * width * cols,
            bytes_accessed=4 * count * length * (pieces * width + cols),
            transcendentals=0,
        ),
    )(table, shared, shared, *grads)


def weigh_far_kernel(table, partial, rows, far_up, far_down, top, bottom):
    half = far_up.shape[0]
    total = partial[0] + dot(rows[0, 0, :half], far_up[...], 0, 0)
    total = (total + dot(rows[0, 0, half:], far_down[...], 0, 0)).astype(jnp.bfloat16)
    half = top.shape[1]
    top[0], bottom[0] = total[:half], total[half:]


def weigh_far(table, partial, shared, grads, start, stop):
    _, _, length, width = shared.shape
    cols = partial.shape[2]
    half = (1, width // 2, cols)
    out = jax.ShapeDtypeStruct((stop - start,) + half[1:], jnp.bfloat16)
    return pl.pallas_call(
        weigh_far_kernel,
        out_shape=(out, out),
        grid_spec=pltpu.PrefetchScalarGridSpec(
            num_scalar_prefetch=1,
            grid=(stop - start,),
            in_specs=[
                pl.BlockSpec((1, width, cols), lambda piece, table: (start + piece, 0, 0)),
                pl.BlockSpec(
                    (1, 1, length, width),
                    lambda piece, table: (2 * table[start + piece] + 1, 1, 0, 0),
                ),
            ]
            + [pl.BlockSpec(grad.shape, lambda piece, table: (0, 0)) for grad in grads],
            out_specs=(pl.BlockSpec(half, lambda piece, table: (piece, 0, 0)),) * 2,
        ),
        compiler_params=pltpu.CompilerParams(vmem_limit_bytes=VMEM_BYTES),
        cost_estimate=pl.CostEstimate(
            flops=2 * (stop - start) * length * width * cols,
            bytes_accessed=(stop - start) * width * (6 * cols + 4 * length),
            transcendentals=0,
        ),
    )(table, partial, shared, *grads)


def terms_kernel(top, bottom, weight, terms):
    half = top.shape[0]
    terms[:half] = dot(top[...], weight[...], 1, 1).astype(jnp.bfloat16)
    terms[half:] = dot(bottom[...], weight[...], 1, 1).astype(jnp.bfloat16)


def row_terms(grads, weight):
    half = grads[0].shape
    rows = 2 * half[0]
    depth, cols = weight.shape
    width = depth // 8
    return pl.pallas_call(
        terms_kernel,
        out_shape=jax.ShapeDtypeStruct((rows, depth), jnp.bfloat16),
        grid=(depth // width,),
        in_specs=[
            pl.BlockSpec(half, lambda block: (0, 0)),
            pl.BlockSpec(half, lambda block: (0, 0)),
            pl.BlockSpec((width, cols), lambda block: (block, 0)),
        ],
        out_specs=pl.BlockSpec((rows, width), lambda block: (0, block)),
        compiler_params=pltpu.CompilerParams(vmem_limit_bytes=VMEM_BYTES),
        cost_estimate=pl.CostEstimate(
            flops=2 * rows * depth * cols,
            bytes_accessed=2 * (rows * cols + depth * (cols + rows)),
            transcendentals=0,
        ),
    )(*grads, weight)


def total_of(*terms):
    return sum(term.astype(jnp.float32) for term in terms).astype(jnp.bfloat16)


def ring_near(block, send):
    return send(block, 1), send(block, -1)


def ring_far(before, after, send):
    half = before.shape[0] // 2
    return send(before[:half], 1), send(after[half:], -1)


def shards(loader_rows, packing, segment_ids, qkv_weight, gain_query, gain_key, out_grad):
    owners = lax.axis_size("row")
    block_count, block_rows, feature_cols = loader_rows.shape
    weight_panel = lax.all_gather(qkv_weight, "row", axis=0, tiled=True)

    col, row = lax.axis_index("col"), lax.axis_index("row")
    y, core = col // 2, col % 2
    x, z = row // N_RING, row % N_RING
    outgoing = pack_blocks(packing, loader_rows, owners)
    arrived = lax.all_to_all(outgoing, "row", split_axis=0, concat_axis=0, tiled=True)
    own_rows = place_blocks(arrived, block_count)
    own_rows = own_rows.reshape(block_count * block_rows, feature_cols)

    half = feature_cols // 2
    left, right = own_rows[:, :half], own_rows[:, half:]
    same, change = jnp.where(z % 2 == 0, left, right), jnp.where(z % 2 == 0, right, left)
    near = ring_near(own_rows, send_y)
    shared = [same, *ring_near(change, send_to_half), send_to_half(same, 2)]
    near, shared = lax.optimization_barrier((near, shared))

    low, high = jnp.stack(shared[:2]), jnp.stack(shared[2:])
    share = jnp.where(
        core == z // 2,
        jnp.where(core == 0, low, high),
        swap_core(jnp.where(core == 0, high, low)),
    )
    far = jnp.concatenate(ring_far(*near, send_y), axis=0)
    far, share = lax.optimization_barrier((far, share))
    own = jnp.stack([own_rows, *near, far])
    other = swap_core(own)
    shared = lax.all_gather(share, "col", axis=0)

    offsets = jnp.array([0, -1, 1, 2], jnp.int32)
    ys = (y + offsets) % N_RING
    order = jnp.concatenate([ys * 2 + core, ys * 2 + 1 - core]).astype(jnp.int32)
    table = ((x - offsets) % N_RING).astype(jnp.int32)
    attn_out, top, bottom = run_heads(
        order, own, other, weight_panel, gain_query, gain_key, segment_ids[0], out_grad
    )

    before_top, after_bottom = send_z(top, 1), send_z(bottom, -1)
    before_bottom, after_top = send_z(bottom, 1), send_z(top, -1)
    near, row_sums = lax.optimization_barrier(
        (
            [before_top, before_bottom, after_top, after_bottom],
            row_terms((top, bottom), weight_panel),
        )
    )
    far, partial = lax.optimization_barrier(
        (
            (send_z(before_top, 1), send_z(after_bottom, -1)),
            weigh_near(table, shared, [top, bottom, *near]),
        )
    )
    tops, bottoms = weigh_far(table, partial, shared, far, 3, 4)
    up, down = send_x(tops[0], 1), send_x(bottoms[0], -1)
    tops, bottoms = weigh_far(table, partial, shared, far, 0, 3)
    after = jnp.concatenate([total_of(tops[1], up), bottoms[1]], axis=0)
    before = jnp.concatenate([tops[2], total_of(bottoms[2], down)], axis=0)
    here = jnp.concatenate([tops[0], bottoms[0]], axis=0)
    grad_weight = total_of(here, send_x(after, 1), send_x(before, -1))
    grad_rows = lax.psum_scatter(row_sums, "col", scatter_dimension=1, tiled=True)
    return (attn_out, grad_rows, grad_weight)


def solution(mesh):
    in_specs = (
        P("row", None, "col"),
        P("row"),
        P("row", None),
        P("row", "col"),
        P("col", None),
        P("col", None),
        P("row", "col"),
    )
    out_specs = (P("row", "col"), P("row", "col"), P("row", "col"))
    return jax.shard_map(shards, mesh=mesh, in_specs=in_specs, out_specs=out_specs, check_vma=False)
```

```python
import jax
import jax.numpy as jnp
from jax import lax
from jax.experimental import pallas as pl
from jax.experimental.pallas import tpu as pltpu
from jax.sharding import PartitionSpec as P

CAP = 2
N_RING = 4
LABEL_COLS = 128
VMEM_BYTES = 56 * 1024 * 1024
SMALL_VMEM_BYTES = 32 * 1024 * 1024


def along_col(dy, dc):
    return [
        (y * 2 + c, ((y + dy) % N_RING) * 2 + (c + dc) % 2) for y in range(N_RING) for c in range(2)
    ]


def along_row(dx, dz):
    return [
        (x * N_RING + z, ((x + dx) % N_RING) * N_RING + (z + dz) % N_RING)
        for x in range(N_RING)
        for z in range(N_RING)
    ]


def send_x(values, step):
    return lax.ppermute(values, "row", along_row(step, 0))


def send_z(values, step):
    return lax.ppermute(values, "row", along_row(0, step))


def send_y(values, step):
    return lax.ppermute(values, "col", along_col(step, 0))


def send_to_half(values, step):
    pairs = []
    for place in range(N_RING * N_RING):
        x, z = divmod(place, N_RING)
        to = (z + step) % N_RING
        for y in range(N_RING):
            col = 2 * y + to // 2
            pairs.append((place * 2 * N_RING + col, (x * N_RING + to) * 2 * N_RING + col))
    return lax.ppermute(values, ("row", "col"), pairs)


def swap_core(values):
    return lax.ppermute(values, "col", along_col(0, 1))


def pack_kernel(packing, blocks, outgoing, source, label, count):
    owners = outgoing.shape[0]
    block_count, block_rows, cols = blocks.shape
    label_rows = block_rows // CAP
    for owner in range(owners):
        count[owner] = 0
    for slot in range(owners * CAP):
        source[slot] = 0
        label[slot] = -1

    def route(block, carry):
        target = packing[block]
        owner = target // block_count
        rank = count[owner]
        count[owner] = rank + 1
        source[owner * CAP + rank] = block
        label[owner * CAP + rank] = target - owner * block_count
        return carry

    lax.fori_loop(0, block_count, route, 0)

    def fill(owner, carry):
        for rank in range(CAP):
            slot = owner * CAP + rank
            outgoing[owner, :, rank * cols : (rank + 1) * cols] = blocks[source[slot]]
            mark = jnp.full((label_rows, LABEL_COLS), label[slot], jnp.int32).astype(jnp.float32)
            outgoing[owner, rank * label_rows : (rank + 1) * label_rows, CAP * cols :] = mark.astype(
                jnp.bfloat16
            )
        return carry

    lax.fori_loop(0, owners, fill, 0)


def pack_blocks(packing, blocks, owners):
    block_count, block_rows, cols = blocks.shape
    return pl.pallas_call(
        pack_kernel,
        out_shape=jax.ShapeDtypeStruct((owners, block_rows, CAP * cols + LABEL_COLS), blocks.dtype),
        in_specs=[
            pl.BlockSpec(memory_space=pltpu.SMEM),
            pl.BlockSpec(memory_space=pltpu.VMEM),
        ],
        out_specs=pl.BlockSpec(memory_space=pltpu.VMEM),
        scratch_shapes=[
            pltpu.SMEM((owners * CAP,), jnp.int32),
            pltpu.SMEM((owners * CAP,), jnp.int32),
            pltpu.SMEM((owners,), jnp.int32),
        ],
        compiler_params=pltpu.CompilerParams(vmem_limit_bytes=VMEM_BYTES),
    )(packing, blocks)


def place_kernel(where, arrived, rows):
    cols = rows.shape[2]

    def place(slot, carry):
        spot = where[slot]
        start = pl.multiple_of((spot % CAP) * cols, cols)
        rows[slot] = arrived[spot // CAP, :, pl.ds(start, cols)]
        return carry

    lax.fori_loop(0, rows.shape[0], place, 0)


def place_blocks(arrived, block_count):
    owners, block_rows, cols = arrived.shape
    cols = (cols - LABEL_COLS) // CAP
    label = arrived[:, :: block_rows // CAP, CAP * cols]
    label = label.astype(jnp.int32).reshape(owners * CAP)
    spots = jnp.arange(owners * CAP, dtype=jnp.int32)
    hit = jnp.arange(block_count, dtype=jnp.int32)[:, None] == label[None, :]
    where = jnp.sum(jnp.where(hit, spots[None, :], 0), axis=1)
    return pl.pallas_call(
        place_kernel,
        out_shape=jax.ShapeDtypeStruct((block_count, block_rows, cols), arrived.dtype),
        in_specs=[
            pl.BlockSpec(memory_space=pltpu.SMEM),
            pl.BlockSpec(memory_space=pltpu.VMEM),
        ],
        out_specs=pl.BlockSpec(memory_space=pltpu.VMEM),
        compiler_params=pltpu.CompilerParams(vmem_limit_bytes=VMEM_BYTES),
    )(where, arrived)


def dot(left, right, left_dim, right_dim):
    return lax.dot_general(
        left, right, (((left_dim,), (right_dim,)), ((), ())), preferred_element_type=jnp.float32
    )


def normalize(values):
    centred = values - jnp.mean(values, axis=-1, keepdims=True)
    inv_std = lax.rsqrt(jnp.mean(centred * centred, axis=-1, keepdims=True) + 1e-06)
    return (centred * inv_std, inv_std)


def norm_grad(upstream, normed, inv_std, gain):
    scaled = upstream * gain
    mean_one = jnp.mean(scaled, axis=-1, keepdims=True)
    mean_two = jnp.mean(scaled * normed, axis=-1, keepdims=True)
    return (scaled - mean_one - normed * mean_two) * inv_std


def attend(projected, gain_query, gain_key, seg_col, seg_row, up):
    size = up.shape[1]
    query_hat, query_inv = normalize(projected[:, :size])
    key_hat, key_inv = normalize(projected[:, size : 2 * size])
    query = (query_hat * gain_query).astype(jnp.bfloat16)
    key = (key_hat * gain_key).astype(jnp.bfloat16)
    value = projected[:, 2 * size :].astype(jnp.bfloat16)
    factor = 1.0 / size**0.5
    weights = jnp.exp(dot(query, key, 1, 1) * factor)
    weights = jnp.where(seg_col == seg_row, weights, 0.0)
    probs = weights * (1.0 / jnp.sum(weights, axis=-1, keepdims=True))
    probs_half = probs.astype(jnp.bfloat16)
    out = dot(probs_half, value, 1, 0).astype(jnp.bfloat16)
    grad_value = dot(probs_half, up, 0, 0)
    grad_probs = dot(up, value, 1, 1)
    inner = jnp.sum(probs * grad_probs, axis=-1, keepdims=True)
    grad_scores = (probs * (grad_probs - inner) * factor).astype(jnp.bfloat16)
    grad_query = norm_grad(dot(grad_scores, key, 1, 0), query_hat, query_inv, gain_query)
    grad_key = norm_grad(dot(grad_scores, query, 0, 0), key_hat, key_inv, gain_key)
    grads = (grad_query, grad_key, grad_value)
    return out, [part.astype(jnp.bfloat16) for part in grads]


def heads_kernel(
    order, own, other, weight, gain_q, gain_k, seg_col, seg_row, upstream, out, top, bottom, total
):
    size = gain_q.shape[-1]
    heads = gain_q.shape[0]
    half = top.shape[0]
    step, blocks = pl.program_id(0), pl.num_programs(0)

    @pl.when(step == 0)
    def _():
        total[...] = jnp.zeros_like(total)

    @pl.when(step < blocks // 2)
    def _():
        total[...] += dot(own[0], weight[...], 1, 0)

    @pl.when(step >= blocks // 2)
    def _():
        total[...] += dot(other[0], weight[...], 1, 0)

    @pl.when(step == blocks - 1)
    def _():
        for head in range(heads):
            left = 3 * head * size
            result, parts = attend(
                total[:, left : left + 3 * size], gain_q[head], gain_k[head],
                seg_col[...], seg_row[...], upstream[:, head * size : (head + 1) * size],
            )
            out[:, head * size : (head + 1) * size] = result
            for kind, part in enumerate(parts):
                span = slice(left + kind * size, left + (kind + 1) * size)
                top[:, span], bottom[:, span] = part[:half], part[half:]


def run_heads(order, own, other, weight, gain_query, gain_key, segments, upstream):
    heads, size = gain_query.shape
    rows = segments.shape[0]
    depth, cols = weight.shape
    blocks = order.shape[0]
    half = blocks // 2
    width = depth // blocks
    fixed = lambda step, order: (0, 0)
    cube = lambda step, order: (0, 0, 0)
    return pl.pallas_call(
        heads_kernel,
        out_shape=(
            jax.ShapeDtypeStruct((rows, heads * size), jnp.bfloat16),
            jax.ShapeDtypeStruct((rows // 2, cols), jnp.bfloat16),
            jax.ShapeDtypeStruct((rows // 2, cols), jnp.bfloat16),
        ),
        grid_spec=pltpu.PrefetchScalarGridSpec(
            num_scalar_prefetch=1,
            grid=(blocks,),
            in_specs=[
                pl.BlockSpec(
                    (1, rows, width), lambda step, order: (jnp.minimum(step, half - 1), 0, 0)
                ),
                pl.BlockSpec(
                    (1, rows, width), lambda step, order: (jnp.maximum(step - half, 0), 0, 0)
                ),
                pl.BlockSpec((width, cols), lambda step, order: (order[step], 0)),
                pl.BlockSpec((heads, 1, size), cube),
                pl.BlockSpec((heads, 1, size), cube),
                pl.BlockSpec((rows, 1), fixed),
                pl.BlockSpec((1, rows), fixed),
                pl.BlockSpec((rows, heads * size), fixed),
            ],
            out_specs=(
                pl.BlockSpec((rows, heads * size), fixed),
                pl.BlockSpec((rows // 2, cols), fixed),
                pl.BlockSpec((rows // 2, cols), fixed),
            ),
            scratch_shapes=[pltpu.VMEM((rows, cols), jnp.float32)],
        ),
        compiler_params=pltpu.CompilerParams(vmem_limit_bytes=VMEM_BYTES),
        cost_estimate=pl.CostEstimate(
            flops=2 * rows * depth * cols,
            bytes_accessed=2 * depth * cols + 2 * rows * depth,
            transcendentals=heads * rows * rows,
        ),
    )(
        order, own, other, weight, gain_query[:, None, :], gain_key[:, None, :],
        segments[:, None], segments[None, :], upstream,
    )


def weigh_near_kernel(table, low, high, *refs):
    grads, terms = refs[:-1], refs[-1]
    half = grads[0].shape[0]
    total = 0.0
    for sequence, rows in enumerate((low[0, 0], low[0, 1], high[0, 0])):
        top, bottom = grads[2 * sequence : 2 * sequence + 2]
        total += dot(rows[:half], top[...], 0, 0) + dot(rows[half:], bottom[...], 0, 0)
    terms[0] = total


def weigh_near(table, shared, grads):
    _, count, length, width = shared.shape
    pieces, cols = table.shape[0], grads[0].shape[1]
    return pl.pallas_call(
        weigh_near_kernel,
        out_shape=jax.ShapeDtypeStruct((pieces, width, cols), jnp.float32),
        grid_spec=pltpu.PrefetchScalarGridSpec(
            num_scalar_prefetch=1,
            grid=(pieces,),
            in_specs=[
                pl.BlockSpec(
                    (1, count, length, width), lambda piece, table: (2 * table[piece], 0, 0, 0)
                ),
                pl.BlockSpec(
                    (1, 1, length, width), lambda piece, table: (2 * table[piece] + 1, 0, 0, 0)
                ),
            ]
            + [pl.BlockSpec(grad.shape, lambda piece, table: (0, 0)) for grad in grads],
            out_specs=pl.BlockSpec((1, width, cols), lambda piece, table: (piece, 0, 0)),
        ),
        compiler_params=pltpu.CompilerParams(vmem_limit_bytes=SMALL_VMEM_BYTES),
        cost_estimate=pl.CostEstimate(
            flops=6 * pieces * length * width * cols,
            bytes_accessed=4 * count * length * (pieces * width + cols),
            transcendentals=0,
        ),
    )(table, shared, shared, *grads)


def weigh_far_kernel(table, partial, rows, far_up, far_down, top, bottom):
    half = far_up.shape[0]
    total = partial[0] + dot(rows[0, 0, :half], far_up[...], 0, 0)
    total = (total + dot(rows[0, 0, half:], far_down[...], 0, 0)).astype(jnp.bfloat16)
    half = top.shape[1]
    top[0], bottom[0] = total[:half], total[half:]


def weigh_far(table, partial, shared, grads, start, stop):
    _, _, length, width = shared.shape
    cols = partial.shape[2]
    half = (1, width // 2, cols)
    out = jax.ShapeDtypeStruct((stop - start,) + half[1:], jnp.bfloat16)
    return pl.pallas_call(
        weigh_far_kernel,
        out_shape=(out, out),
        grid_spec=pltpu.PrefetchScalarGridSpec(
            num_scalar_prefetch=1,
            grid=(stop - start,),
            in_specs=[
                pl.BlockSpec((1, width, cols), lambda piece, table: (start + piece, 0, 0)),
                pl.BlockSpec(
                    (1, 1, length, width),
                    lambda piece, table: (2 * table[start + piece] + 1, 1, 0, 0),
                ),
            ]
            + [pl.BlockSpec(grad.shape, lambda piece, table: (0, 0)) for grad in grads],
            out_specs=(pl.BlockSpec(half, lambda piece, table: (piece, 0, 0)),) * 2,
        ),
        compiler_params=pltpu.CompilerParams(vmem_limit_bytes=SMALL_VMEM_BYTES),
        cost_estimate=pl.CostEstimate(
            flops=2 * (stop - start) * length * width * cols,
            bytes_accessed=(stop - start) * width * (6 * cols + 4 * length),
            transcendentals=0,
        ),
    )(table, partial, shared, *grads)


def terms_kernel(top, bottom, weight, terms):
    half = top.shape[0]
    terms[:half] = dot(top[...], weight[...], 1, 1).astype(jnp.bfloat16)
    terms[half:] = dot(bottom[...], weight[...], 1, 1).astype(jnp.bfloat16)


def row_terms(grads, weight):
    half = grads[0].shape
    rows = 2 * half[0]
    depth, cols = weight.shape
    width = depth // 8
    return pl.pallas_call(
        terms_kernel,
        out_shape=jax.ShapeDtypeStruct((rows, depth), jnp.bfloat16),
        grid=(depth // width,),
        in_specs=[
            pl.BlockSpec(half, lambda block: (0, 0)),
            pl.BlockSpec(half, lambda block: (0, 0)),
            pl.BlockSpec((width, cols), lambda block: (block, 0)),
        ],
        out_specs=pl.BlockSpec((rows, width), lambda block: (0, block)),
        compiler_params=pltpu.CompilerParams(vmem_limit_bytes=VMEM_BYTES),
        cost_estimate=pl.CostEstimate(
            flops=2 * rows * depth * cols,
            bytes_accessed=2 * (rows * cols + depth * (cols + rows)),
            transcendentals=0,
        ),
    )(*grads, weight)


def total_of(*terms):
    return sum(term.astype(jnp.float32) for term in terms).astype(jnp.bfloat16)


def ring_near(block, send):
    return send(block, 1), send(block, -1)


def ring_far(before, after, send):
    half = before.shape[0] // 2
    return send(before[:half], 1), send(after[half:], -1)


def shards(loader_rows, packing, segment_ids, qkv_weight, gain_query, gain_key, out_grad):
    owners = lax.axis_size("row")
    block_count, block_rows, feature_cols = loader_rows.shape
    weight_panel = lax.all_gather(qkv_weight, "row", axis=0, tiled=True)

    col, row = lax.axis_index("col"), lax.axis_index("row")
    y, core = col // 2, col % 2
    x, z = row // N_RING, row % N_RING
    outgoing = pack_blocks(packing, loader_rows, owners)
    arrived = lax.all_to_all(outgoing, "row", split_axis=0, concat_axis=0, tiled=True)
    own_rows = place_blocks(arrived, block_count)
    own_rows = own_rows.reshape(block_count * block_rows, feature_cols)

    half = feature_cols // 2
    left, right = own_rows[:, :half], own_rows[:, half:]
    same, change = jnp.where(z % 2 == 0, left, right), jnp.where(z % 2 == 0, right, left)
    near = ring_near(own_rows, send_y)
    shared = [same, *ring_near(change, send_to_half), send_to_half(same, 2)]
    near, shared = lax.optimization_barrier((near, shared))

    low, high = jnp.stack(shared[:2]), jnp.stack(shared[2:])
    share = jnp.where(
        core == z // 2,
        jnp.where(core == 0, low, high),
        swap_core(jnp.where(core == 0, high, low)),
    )
    far = jnp.concatenate(ring_far(*near, send_y), axis=0)
    far, share = lax.optimization_barrier((far, share))
    own = jnp.stack([own_rows, *near, far])
    other = swap_core(own)
    shared = lax.all_gather(share, "col", axis=0)

    offsets = jnp.array([0, -1, 1, 2], jnp.int32)
    ys = (y + offsets) % N_RING
    order = jnp.concatenate([ys * 2 + core, ys * 2 + 1 - core]).astype(jnp.int32)
    table = ((x - offsets) % N_RING).astype(jnp.int32)
    attn_out, top, bottom = run_heads(
        order, own, other, weight_panel, gain_query, gain_key, segment_ids[0], out_grad
    )

    before_top, after_bottom = send_z(top, 1), send_z(bottom, -1)
    before_bottom, after_top = send_z(bottom, 1), send_z(top, -1)
    near, row_sums = lax.optimization_barrier(
        (
            [before_top, before_bottom, after_top, after_bottom],
            row_terms((top, bottom), weight_panel),
        )
    )
    far, partial = lax.optimization_barrier(
        (
            (send_z(before_top, 1), send_z(after_bottom, -1)),
            weigh_near(table, shared, [top, bottom, *near]),
        )
    )
    tops, bottoms = weigh_far(table, partial, shared, far, 3, 4)
    up, down = send_x(tops[0], 1), send_x(bottoms[0], -1)
    tops, bottoms = weigh_far(table, partial, shared, far, 0, 3)
    after = jnp.concatenate([total_of(tops[1], up), bottoms[1]], axis=0)
    before = jnp.concatenate([tops[2], total_of(bottoms[2], down)], axis=0)
    here = jnp.concatenate([tops[0], bottoms[0]], axis=0)
    grad_weight = total_of(here, send_x(after, 1), send_x(before, -1))
    grad_rows = lax.psum_scatter(row_sums, "col", scatter_dimension=1, tiled=True)
    return (attn_out, grad_rows, grad_weight)


def solution(mesh):
    in_specs = (
        P("row", None, "col"),
        P("row"),
        P("row", None),
        P("row", "col"),
        P("col", None),
        P("col", None),
        P("row", "col"),
    )
    out_specs = (P("row", "col"), P("row", "col"), P("row", "col"))
    return jax.shard_map(shards, mesh=mesh, in_specs=in_specs, out_specs=out_specs, check_vma=False)
```

```python
import jax
import jax.numpy as jnp
from jax import lax
from jax.experimental import pallas as pl
from jax.experimental.pallas import tpu as pltpu
from jax.sharding import PartitionSpec as P

CAP = 2
N_RING = 4
LABEL_COLS = 128
VMEM_BYTES = 56 * 1024 * 1024
SMALL_VMEM_BYTES = 32 * 1024 * 1024


def along_col(dy, dc):
    return [
        (y * 2 + c, ((y + dy) % N_RING) * 2 + (c + dc) % 2) for y in range(N_RING) for c in range(2)
    ]


def along_row(dx, dz):
    return [
        (x * N_RING + z, ((x + dx) % N_RING) * N_RING + (z + dz) % N_RING)
        for x in range(N_RING)
        for z in range(N_RING)
    ]


def send_x(values, step):
    return lax.ppermute(values, "row", along_row(step, 0))


def send_z(values, step):
    return lax.ppermute(values, "row", along_row(0, step))


def send_y(values, step):
    return lax.ppermute(values, "col", along_col(step, 0))


def send_to_half(values, step):
    pairs = []
    for place in range(N_RING * N_RING):
        x, z = divmod(place, N_RING)
        to = (z + step) % N_RING
        for y in range(N_RING):
            col = 2 * y + to // 2
            pairs.append((place * 2 * N_RING + col, (x * N_RING + to) * 2 * N_RING + col))
    return lax.ppermute(values, ("row", "col"), pairs)


def swap_core(values):
    return lax.ppermute(values, "col", along_col(0, 1))


def pack_kernel(packing, blocks, outgoing, source, label, count):
    owners = outgoing.shape[0]
    block_count, block_rows, cols = blocks.shape
    label_rows = block_rows // CAP
    for owner in range(owners):
        count[owner] = 0
    for slot in range(owners * CAP):
        source[slot] = 0
        label[slot] = -1

    def route(block, carry):
        target = packing[block]
        owner = target // block_count
        rank = count[owner]
        count[owner] = rank + 1
        source[owner * CAP + rank] = block
        label[owner * CAP + rank] = target - owner * block_count
        return carry

    lax.fori_loop(0, block_count, route, 0)

    def fill(owner, carry):
        for rank in range(CAP):
            slot = owner * CAP + rank
            outgoing[owner, :, rank * cols : (rank + 1) * cols] = blocks[source[slot]]
            mark = jnp.full((label_rows, LABEL_COLS), label[slot], jnp.int32).astype(jnp.float32)
            outgoing[owner, rank * label_rows : (rank + 1) * label_rows, CAP * cols :] = mark.astype(
                jnp.bfloat16
            )
        return carry

    lax.fori_loop(0, owners, fill, 0)


def pack_blocks(packing, blocks, owners):
    block_count, block_rows, cols = blocks.shape
    return pl.pallas_call(
        pack_kernel,
        out_shape=jax.ShapeDtypeStruct((owners, block_rows, CAP * cols + LABEL_COLS), blocks.dtype),
        in_specs=[
            pl.BlockSpec(memory_space=pltpu.SMEM),
            pl.BlockSpec(memory_space=pltpu.VMEM),
        ],
        out_specs=pl.BlockSpec(memory_space=pltpu.VMEM),
        scratch_shapes=[
            pltpu.SMEM((owners * CAP,), jnp.int32),
            pltpu.SMEM((owners * CAP,), jnp.int32),
            pltpu.SMEM((owners,), jnp.int32),
        ],
        compiler_params=pltpu.CompilerParams(vmem_limit_bytes=VMEM_BYTES),
    )(packing, blocks)


def place_kernel(where, arrived, rows):
    cols = rows.shape[2]

    def place(slot, carry):
        spot = where[slot]
        start = pl.multiple_of((spot % CAP) * cols, cols)
        rows[slot] = arrived[spot // CAP, :, pl.ds(start, cols)]
        return carry

    lax.fori_loop(0, rows.shape[0], place, 0)


def place_blocks(arrived, block_count):
    owners, block_rows, cols = arrived.shape
    cols = (cols - LABEL_COLS) // CAP
    label = arrived[:, :: block_rows // CAP, CAP * cols]
    label = label.astype(jnp.int32).reshape(owners * CAP)
    spots = jnp.arange(owners * CAP, dtype=jnp.int32)
    hit = jnp.arange(block_count, dtype=jnp.int32)[:, None] == label[None, :]
    where = jnp.sum(jnp.where(hit, spots[None, :], 0), axis=1)
    return pl.pallas_call(
        place_kernel,
        out_shape=jax.ShapeDtypeStruct((block_count, block_rows, cols), arrived.dtype),
        in_specs=[
            pl.BlockSpec(memory_space=pltpu.SMEM),
            pl.BlockSpec(memory_space=pltpu.VMEM),
        ],
        out_specs=pl.BlockSpec(memory_space=pltpu.VMEM),
        compiler_params=pltpu.CompilerParams(vmem_limit_bytes=VMEM_BYTES),
    )(where, arrived)


def dot(left, right, left_dim, right_dim):
    return lax.dot_general(
        left, right, (((left_dim,), (right_dim,)), ((), ())), preferred_element_type=jnp.float32
    )


def normalize(values):
    centred = values - jnp.mean(values, axis=-1, keepdims=True)
    inv_std = lax.rsqrt(jnp.mean(centred * centred, axis=-1, keepdims=True) + 1e-06)
    return (centred * inv_std, inv_std)


def norm_grad(upstream, normed, inv_std, gain):
    scaled = upstream * gain
    mean_one = jnp.mean(scaled, axis=-1, keepdims=True)
    mean_two = jnp.mean(scaled * normed, axis=-1, keepdims=True)
    return (scaled - mean_one - normed * mean_two) * inv_std


def attend(projected, gain_query, gain_key, seg_col, seg_row, up):
    size = up.shape[1]
    query_hat, query_inv = normalize(projected[:, :size])
    key_hat, key_inv = normalize(projected[:, size : 2 * size])
    query = (query_hat * gain_query).astype(jnp.bfloat16)
    key = (key_hat * gain_key).astype(jnp.bfloat16)
    value = projected[:, 2 * size :].astype(jnp.bfloat16)
    factor = 1.0 / size**0.5
    weights = jnp.exp(dot(query, key, 1, 1) * factor)
    weights = jnp.where(seg_col == seg_row, weights, 0.0)
    probs = weights * (1.0 / jnp.sum(weights, axis=-1, keepdims=True))
    probs_half = probs.astype(jnp.bfloat16)
    out = dot(probs_half, value, 1, 0)
    grad_value = dot(probs_half, up, 0, 0)
    grad_probs = dot(up, value, 1, 1)
    inner = jnp.sum(up.astype(jnp.float32) * out, axis=-1, keepdims=True)
    grad_scores = (probs * (grad_probs - inner) * factor).astype(jnp.bfloat16)
    grad_query = norm_grad(dot(grad_scores, key, 1, 0), query_hat, query_inv, gain_query)
    grad_key = norm_grad(dot(grad_scores, query, 0, 0), key_hat, key_inv, gain_key)
    grads = (grad_query, grad_key, grad_value)
    return out.astype(jnp.bfloat16), [part.astype(jnp.bfloat16) for part in grads]


def heads_kernel(
    order, own, other, weight, gain_q, gain_k, seg_col, seg_row, upstream, out, top, bottom, total
):
    size = gain_q.shape[-1]
    heads = gain_q.shape[0]
    half = top.shape[0]
    step, blocks = pl.program_id(0), pl.num_programs(0)

    @pl.when(step == 0)
    def _():
        total[...] = jnp.zeros_like(total)

    @pl.when(step < blocks // 2)
    def _():
        total[...] += dot(own[0], weight[...], 1, 0)

    @pl.when(step >= blocks // 2)
    def _():
        total[...] += dot(other[0], weight[...], 1, 0)

    @pl.when(step == blocks - 1)
    def _():
        for head in range(heads):
            left = 3 * head * size
            result, parts = attend(
                total[:, left : left + 3 * size], gain_q[head], gain_k[head],
                seg_col[...], seg_row[...], upstream[:, head * size : (head + 1) * size],
            )
            out[:, head * size : (head + 1) * size] = result
            for kind, part in enumerate(parts):
                span = slice(left + kind * size, left + (kind + 1) * size)
                top[:, span], bottom[:, span] = part[:half], part[half:]


def run_heads(order, own, other, weight, gain_query, gain_key, segments, upstream):
    heads, size = gain_query.shape
    rows = segments.shape[0]
    depth, cols = weight.shape
    blocks = order.shape[0]
    half = blocks // 2
    width = depth // blocks
    fixed = lambda step, order: (0, 0)
    cube = lambda step, order: (0, 0, 0)
    return pl.pallas_call(
        heads_kernel,
        out_shape=(
            jax.ShapeDtypeStruct((rows, heads * size), jnp.bfloat16),
            jax.ShapeDtypeStruct((rows // 2, cols), jnp.bfloat16),
            jax.ShapeDtypeStruct((rows // 2, cols), jnp.bfloat16),
        ),
        grid_spec=pltpu.PrefetchScalarGridSpec(
            num_scalar_prefetch=1,
            grid=(blocks,),
            in_specs=[
                pl.BlockSpec(
                    (1, rows, width), lambda step, order: (jnp.minimum(step, half - 1), 0, 0)
                ),
                pl.BlockSpec(
                    (1, rows, width), lambda step, order: (jnp.maximum(step - half, 0), 0, 0)
                ),
                pl.BlockSpec((width, cols), lambda step, order: (order[step], 0)),
                pl.BlockSpec((heads, 1, size), cube),
                pl.BlockSpec((heads, 1, size), cube),
                pl.BlockSpec((rows, 1), fixed),
                pl.BlockSpec((1, rows), fixed),
                pl.BlockSpec((rows, heads * size), fixed),
            ],
            out_specs=(
                pl.BlockSpec((rows, heads * size), fixed),
                pl.BlockSpec((rows // 2, cols), fixed),
                pl.BlockSpec((rows // 2, cols), fixed),
            ),
            scratch_shapes=[pltpu.VMEM((rows, cols), jnp.float32)],
        ),
        compiler_params=pltpu.CompilerParams(vmem_limit_bytes=VMEM_BYTES),
        cost_estimate=pl.CostEstimate(
            flops=2 * rows * depth * cols,
            bytes_accessed=2 * depth * cols + 2 * rows * depth,
            transcendentals=heads * rows * rows,
        ),
    )(
        order, own, other, weight, gain_query[:, None, :], gain_key[:, None, :],
        segments[:, None], segments[None, :], upstream,
    )


def weigh_near_kernel(table, low, high, *refs):
    grads, terms = refs[:-1], refs[-1]
    half = grads[0].shape[0]
    total = 0.0
    for sequence, rows in enumerate((low[0, 0], low[0, 1], high[0, 0])):
        top, bottom = grads[2 * sequence : 2 * sequence + 2]
        total += dot(rows[:half], top[...], 0, 0) + dot(rows[half:], bottom[...], 0, 0)
    terms[0] = total


def weigh_near(table, shared, grads):
    _, count, length, width = shared.shape
    pieces, cols = table.shape[0], grads[0].shape[1]
    return pl.pallas_call(
        weigh_near_kernel,
        out_shape=jax.ShapeDtypeStruct((pieces, width, cols), jnp.float32),
        grid_spec=pltpu.PrefetchScalarGridSpec(
            num_scalar_prefetch=1,
            grid=(pieces,),
            in_specs=[
                pl.BlockSpec(
                    (1, count, length, width), lambda piece, table: (2 * table[piece], 0, 0, 0)
                ),
                pl.BlockSpec(
                    (1, 1, length, width), lambda piece, table: (2 * table[piece] + 1, 0, 0, 0)
                ),
            ]
            + [pl.BlockSpec(grad.shape, lambda piece, table: (0, 0)) for grad in grads],
            out_specs=pl.BlockSpec((1, width, cols), lambda piece, table: (piece, 0, 0)),
        ),
        compiler_params=pltpu.CompilerParams(vmem_limit_bytes=SMALL_VMEM_BYTES),
        cost_estimate=pl.CostEstimate(
            flops=6 * pieces * length * width * cols,
            bytes_accessed=4 * count * length * (pieces * width + cols),
            transcendentals=0,
        ),
    )(table, shared, shared, *grads)


def weigh_far_kernel(table, partial, rows, far_up, far_down, top, bottom):
    half = far_up.shape[0]
    total = partial[0] + dot(rows[0, 0, :half], far_up[...], 0, 0)
    total = (total + dot(rows[0, 0, half:], far_down[...], 0, 0)).astype(jnp.bfloat16)
    half = top.shape[1]
    top[0], bottom[0] = total[:half], total[half:]


def weigh_far(table, partial, shared, grads, start, stop):
    _, _, length, width = shared.shape
    cols = partial.shape[2]
    half = (1, width // 2, cols)
    out = jax.ShapeDtypeStruct((stop - start,) + half[1:], jnp.bfloat16)
    return pl.pallas_call(
        weigh_far_kernel,
        out_shape=(out, out),
        grid_spec=pltpu.PrefetchScalarGridSpec(
            num_scalar_prefetch=1,
            grid=(stop - start,),
            in_specs=[
                pl.BlockSpec((1, width, cols), lambda piece, table: (start + piece, 0, 0)),
                pl.BlockSpec(
                    (1, 1, length, width),
                    lambda piece, table: (2 * table[start + piece] + 1, 1, 0, 0),
                ),
            ]
            + [pl.BlockSpec(grad.shape, lambda piece, table: (0, 0)) for grad in grads],
            out_specs=(pl.BlockSpec(half, lambda piece, table: (piece, 0, 0)),) * 2,
        ),
        compiler_params=pltpu.CompilerParams(vmem_limit_bytes=SMALL_VMEM_BYTES),
        cost_estimate=pl.CostEstimate(
            flops=2 * (stop - start) * length * width * cols,
            bytes_accessed=(stop - start) * width * (6 * cols + 4 * length),
            transcendentals=0,
        ),
    )(table, partial, shared, *grads)


def terms_kernel(top, bottom, weight, terms):
    half = top.shape[0]
    terms[:half] = dot(top[...], weight[...], 1, 1).astype(jnp.bfloat16)
    terms[half:] = dot(bottom[...], weight[...], 1, 1).astype(jnp.bfloat16)


def row_terms(grads, weight):
    half = grads[0].shape
    rows = 2 * half[0]
    depth, cols = weight.shape
    width = depth // 8
    return pl.pallas_call(
        terms_kernel,
        out_shape=jax.ShapeDtypeStruct((rows, depth), jnp.bfloat16),
        grid=(depth // width,),
        in_specs=[
            pl.BlockSpec(half, lambda block: (0, 0)),
            pl.BlockSpec(half, lambda block: (0, 0)),
            pl.BlockSpec((width, cols), lambda block: (block, 0)),
        ],
        out_specs=pl.BlockSpec((rows, width), lambda block: (0, block)),
        compiler_params=pltpu.CompilerParams(vmem_limit_bytes=VMEM_BYTES),
        cost_estimate=pl.CostEstimate(
            flops=2 * rows * depth * cols,
            bytes_accessed=2 * (rows * cols + depth * (cols + rows)),
            transcendentals=0,
        ),
    )(*grads, weight)


def total_of(*terms):
    return sum(term.astype(jnp.float32) for term in terms).astype(jnp.bfloat16)


def ring_near(block, send):
    return send(block, 1), send(block, -1)


def ring_far(before, after, send):
    half = before.shape[0] // 2
    return send(before[:half], 1), send(after[half:], -1)


def shards(loader_rows, packing, segment_ids, qkv_weight, gain_query, gain_key, out_grad):
    owners = lax.axis_size("row")
    block_count, block_rows, feature_cols = loader_rows.shape
    weight_panel = lax.all_gather(qkv_weight, "row", axis=0, tiled=True)

    col, row = lax.axis_index("col"), lax.axis_index("row")
    y, core = col // 2, col % 2
    x, z = row // N_RING, row % N_RING
    outgoing = pack_blocks(packing, loader_rows, owners)
    arrived = lax.all_to_all(outgoing, "row", split_axis=0, concat_axis=0, tiled=True)
    own_rows = place_blocks(arrived, block_count)
    own_rows = own_rows.reshape(block_count * block_rows, feature_cols)

    half = feature_cols // 2
    left, right = own_rows[:, :half], own_rows[:, half:]
    same, change = jnp.where(z % 2 == 0, left, right), jnp.where(z % 2 == 0, right, left)
    near = ring_near(own_rows, send_y)
    shared = [same, *ring_near(change, send_to_half), send_to_half(same, 2)]
    near, shared = lax.optimization_barrier((near, shared))

    low, high = jnp.stack(shared[:2]), jnp.stack(shared[2:])
    share = jnp.where(
        core == z // 2,
        jnp.where(core == 0, low, high),
        swap_core(jnp.where(core == 0, high, low)),
    )
    far = jnp.concatenate(ring_far(*near, send_y), axis=0)
    far, share = lax.optimization_barrier((far, share))
    own = jnp.stack([own_rows, *near, far])
    other = swap_core(own)
    shared = lax.all_gather(share, "col", axis=0)

    offsets = jnp.array([0, -1, 1, 2], jnp.int32)
    ys = (y + offsets) % N_RING
    order = jnp.concatenate([ys * 2 + core, ys * 2 + 1 - core]).astype(jnp.int32)
    table = ((x - offsets) % N_RING).astype(jnp.int32)
    attn_out, top, bottom = run_heads(
        order, own, other, weight_panel, gain_query, gain_key, segment_ids[0], out_grad
    )

    before_top, after_bottom = send_z(top, 1), send_z(bottom, -1)
    before_bottom, after_top = send_z(bottom, 1), send_z(top, -1)
    near, row_sums = lax.optimization_barrier(
        (
            [before_top, before_bottom, after_top, after_bottom],
            row_terms((top, bottom), weight_panel),
        )
    )
    far, partial = lax.optimization_barrier(
        (
            (send_z(before_top, 1), send_z(after_bottom, -1)),
            weigh_near(table, shared, [top, bottom, *near]),
        )
    )
    tops, bottoms = weigh_far(table, partial, shared, far, 3, 4)
    up, down = send_x(tops[0], 1), send_x(bottoms[0], -1)
    tops, bottoms = weigh_far(table, partial, shared, far, 0, 3)
    after = jnp.concatenate([total_of(tops[1], up), bottoms[1]], axis=0)
    before = jnp.concatenate([tops[2], total_of(bottoms[2], down)], axis=0)
    here = jnp.concatenate([tops[0], bottoms[0]], axis=0)
    grad_weight = total_of(here, send_x(after, 1), send_x(before, -1))
    grad_rows = lax.psum_scatter(row_sums, "col", scatter_dimension=1, tiled=True)
    return (attn_out, grad_rows, grad_weight)


def solution(mesh):
    in_specs = (
        P("row", None, "col"),
        P("row"),
        P("row", None),
        P("row", "col"),
        P("col", None),
        P("col", None),
        P("row", "col"),
    )
    out_specs = (P("row", "col"), P("row", "col"), P("row", "col"))
    return jax.shard_map(shards, mesh=mesh, in_specs=in_specs, out_specs=out_specs, check_vma=False)
```

```python
import jax
import jax.numpy as jnp
from jax import lax
from jax.experimental import pallas as pl
from jax.experimental.pallas import tpu as pltpu
from jax.sharding import PartitionSpec as P

CAP = 2
N_RING = 4
LABEL_COLS = 128
VMEM_BYTES = 56 * 1024 * 1024
SMALL_VMEM_BYTES = 32 * 1024 * 1024


def along_col(dy, dc):
    return [
        (y * 2 + c, ((y + dy) % N_RING) * 2 + (c + dc) % 2) for y in range(N_RING) for c in range(2)
    ]


def along_row(dx, dz):
    return [
        (x * N_RING + z, ((x + dx) % N_RING) * N_RING + (z + dz) % N_RING)
        for x in range(N_RING)
        for z in range(N_RING)
    ]


def send_x(values, step):
    return lax.ppermute(values, "row", along_row(step, 0))


def send_z(values, step):
    return lax.ppermute(values, "row", along_row(0, step))


def send_y(values, step):
    return lax.ppermute(values, "col", along_col(step, 0))


def share_z(values, near):
    pairs = []
    for x in range(N_RING):
        for z in range(N_RING):
            for y in range(N_RING):
                for core in range(2):
                    step = (1, 3) if near else (0, 2)
                    slot = [(z + d) % N_RING // 2 for d in step].index(core)
                    to = (z + step[slot]) % N_RING
                    source = (x * N_RING + z) * 2 * N_RING + 2 * y + core
                    pairs.append((source, (x * N_RING + to) * 2 * N_RING + 2 * y + slot))
    return lax.ppermute(values, ("row", "col"), pairs)


def swap_core(values):
    return lax.ppermute(values, "col", along_col(0, 1))


def pack_kernel(packing, blocks, outgoing, source, label, count):
    owners = outgoing.shape[0]
    block_count, block_rows, cols = blocks.shape
    label_rows = block_rows // CAP
    for owner in range(owners):
        count[owner] = 0
    for slot in range(owners * CAP):
        source[slot] = 0
        label[slot] = -1

    def route(block, carry):
        target = packing[block]
        owner = target // block_count
        rank = count[owner]
        count[owner] = rank + 1
        source[owner * CAP + rank] = block
        label[owner * CAP + rank] = target - owner * block_count
        return carry

    lax.fori_loop(0, block_count, route, 0)

    def fill(owner, carry):
        for rank in range(CAP):
            slot = owner * CAP + rank
            outgoing[owner, :, rank * cols : (rank + 1) * cols] = blocks[source[slot]]
            mark = jnp.full((label_rows, LABEL_COLS), label[slot], jnp.int32).astype(jnp.float32)
            outgoing[owner, rank * label_rows : (rank + 1) * label_rows, CAP * cols :] = mark.astype(
                jnp.bfloat16
            )
        return carry

    lax.fori_loop(0, owners, fill, 0)


def pack_blocks(packing, blocks, owners):
    block_count, block_rows, cols = blocks.shape
    return pl.pallas_call(
        pack_kernel,
        out_shape=jax.ShapeDtypeStruct((owners, block_rows, CAP * cols + LABEL_COLS), blocks.dtype),
        in_specs=[
            pl.BlockSpec(memory_space=pltpu.SMEM),
            pl.BlockSpec(memory_space=pltpu.VMEM),
        ],
        out_specs=pl.BlockSpec(memory_space=pltpu.VMEM),
        scratch_shapes=[
            pltpu.SMEM((owners * CAP,), jnp.int32),
            pltpu.SMEM((owners * CAP,), jnp.int32),
            pltpu.SMEM((owners,), jnp.int32),
        ],
        compiler_params=pltpu.CompilerParams(vmem_limit_bytes=VMEM_BYTES),
    )(packing, blocks)


def place_kernel(where, arrived, rows):
    cols = rows.shape[2]

    def place(slot, carry):
        spot = where[slot]
        start = pl.multiple_of((spot % CAP) * cols, cols)
        rows[slot] = arrived[spot // CAP, :, pl.ds(start, cols)]
        return carry

    lax.fori_loop(0, rows.shape[0], place, 0)


def place_blocks(arrived, block_count):
    owners, block_rows, cols = arrived.shape
    cols = (cols - LABEL_COLS) // CAP
    label = arrived[:, :: block_rows // CAP, CAP * cols]
    label = label.astype(jnp.int32).reshape(owners * CAP)
    spots = jnp.arange(owners * CAP, dtype=jnp.int32)
    hit = jnp.arange(block_count, dtype=jnp.int32)[:, None] == label[None, :]
    where = jnp.sum(jnp.where(hit, spots[None, :], 0), axis=1)
    return pl.pallas_call(
        place_kernel,
        out_shape=jax.ShapeDtypeStruct((block_count, block_rows, cols), arrived.dtype),
        in_specs=[
            pl.BlockSpec(memory_space=pltpu.SMEM),
            pl.BlockSpec(memory_space=pltpu.VMEM),
        ],
        out_specs=pl.BlockSpec(memory_space=pltpu.VMEM),
        compiler_params=pltpu.CompilerParams(vmem_limit_bytes=VMEM_BYTES),
    )(where, arrived)


def dot(left, right, left_dim, right_dim):
    return lax.dot_general(
        left, right, (((left_dim,), (right_dim,)), ((), ())), preferred_element_type=jnp.float32
    )


def normalize(values):
    centred = values - jnp.mean(values, axis=-1, keepdims=True)
    inv_std = lax.rsqrt(jnp.mean(centred * centred, axis=-1, keepdims=True) + 1e-06)
    return (centred * inv_std, inv_std)


def norm_grad(upstream, normed, inv_std, gain):
    scaled = upstream * gain
    mean_one = jnp.mean(scaled, axis=-1, keepdims=True)
    mean_two = jnp.mean(scaled * normed, axis=-1, keepdims=True)
    return (scaled - mean_one - normed * mean_two) * inv_std


def attend(projected, gain_query, gain_key, seg_col, seg_row, up):
    size = up.shape[1]
    query_hat, query_inv = normalize(projected[:, :size])
    key_hat, key_inv = normalize(projected[:, size : 2 * size])
    query = (query_hat * gain_query).astype(jnp.bfloat16)
    key = (key_hat * gain_key).astype(jnp.bfloat16)
    value = projected[:, 2 * size :].astype(jnp.bfloat16)
    factor = 1.0 / size**0.5
    weights = jnp.exp(dot(query, key, 1, 1) * factor)
    weights = jnp.where(seg_col == seg_row, weights, 0.0)
    probs = weights * (1.0 / jnp.sum(weights, axis=-1, keepdims=True))
    probs_half = probs.astype(jnp.bfloat16)
    out = dot(probs_half, value, 1, 0).astype(jnp.bfloat16)
    grad_value = dot(probs_half, up, 0, 0)
    grad_probs = dot(up, value, 1, 1)
    inner = jnp.sum(probs * grad_probs, axis=-1, keepdims=True)
    grad_scores = (probs * (grad_probs - inner) * factor).astype(jnp.bfloat16)
    grad_query = norm_grad(dot(grad_scores, key, 1, 0), query_hat, query_inv, gain_query)
    grad_key = norm_grad(dot(grad_scores, query, 0, 0), key_hat, key_inv, gain_key)
    grads = (grad_query, grad_key, grad_value)
    return out, [part.astype(jnp.bfloat16) for part in grads]


def heads_kernel(
    order, own, other, weight, gain_q, gain_k, seg_col, seg_row, upstream, out, top, bottom, total
):
    size = gain_q.shape[-1]
    heads = gain_q.shape[0]
    half = top.shape[0]
    step, blocks = pl.program_id(0), pl.num_programs(0)

    @pl.when(step == 0)
    def _():
        total[...] = jnp.zeros_like(total)

    @pl.when(step < blocks // 2)
    def _():
        total[...] += dot(own[0], weight[...], 1, 0)

    @pl.when(step >= blocks // 2)
    def _():
        total[...] += dot(other[0], weight[...], 1, 0)

    @pl.when(step == blocks - 1)
    def _():
        for head in range(heads):
            left = 3 * head * size
            result, parts = attend(
                total[:, left : left + 3 * size], gain_q[head], gain_k[head],
                seg_col[...], seg_row[...], upstream[:, head * size : (head + 1) * size],
            )
            out[:, head * size : (head + 1) * size] = result
            for kind, part in enumerate(parts):
                span = slice(left + kind * size, left + (kind + 1) * size)
                top[:, span], bottom[:, span] = part[:half], part[half:]


def run_heads(order, own, other, weight, gain_query, gain_key, segments, upstream):
    heads, size = gain_query.shape
    rows = segments.shape[0]
    depth, cols = weight.shape
    blocks = order.shape[0]
    half = blocks // 2
    width = depth // blocks
    fixed = lambda step, order: (0, 0)
    cube = lambda step, order: (0, 0, 0)
    return pl.pallas_call(
        heads_kernel,
        out_shape=(
            jax.ShapeDtypeStruct((rows, heads * size), jnp.bfloat16),
            jax.ShapeDtypeStruct((rows // 2, cols), jnp.bfloat16),
            jax.ShapeDtypeStruct((rows // 2, cols), jnp.bfloat16),
        ),
        grid_spec=pltpu.PrefetchScalarGridSpec(
            num_scalar_prefetch=1,
            grid=(blocks,),
            in_specs=[
                pl.BlockSpec(
                    (1, rows, width), lambda step, order: (jnp.minimum(step, half - 1), 0, 0)
                ),
                pl.BlockSpec(
                    (1, rows, width), lambda step, order: (jnp.maximum(step - half, 0), 0, 0)
                ),
                pl.BlockSpec((width, cols), lambda step, order: (order[step], 0)),
                pl.BlockSpec((heads, 1, size), cube),
                pl.BlockSpec((heads, 1, size), cube),
                pl.BlockSpec((rows, 1), fixed),
                pl.BlockSpec((1, rows), fixed),
                pl.BlockSpec((rows, heads * size), fixed),
            ],
            out_specs=(
                pl.BlockSpec((rows, heads * size), fixed),
                pl.BlockSpec((rows // 2, cols), fixed),
                pl.BlockSpec((rows // 2, cols), fixed),
            ),
            scratch_shapes=[pltpu.VMEM((rows, cols), jnp.float32)],
        ),
        compiler_params=pltpu.CompilerParams(vmem_limit_bytes=VMEM_BYTES),
        cost_estimate=pl.CostEstimate(
            flops=2 * rows * depth * cols,
            bytes_accessed=2 * depth * cols + 2 * rows * depth,
            transcendentals=heads * rows * rows,
        ),
    )(
        order, own, other, weight, gain_query[:, None, :], gain_key[:, None, :],
        segments[:, None], segments[None, :], upstream,
    )


def weigh_near_kernel(table, low, high, *refs):
    grads, terms = refs[:-1], refs[-1]
    half = grads[0].shape[0]
    total = 0.0
    for sequence, rows in enumerate((low[0, 1], low[0, 0], high[0, 0])):
        top, bottom = grads[2 * sequence : 2 * sequence + 2]
        total += dot(rows[:half], top[...], 0, 0) + dot(rows[half:], bottom[...], 0, 0)
    terms[0] = total


def weigh_near(table, shared, grads):
    _, count, length, width = shared.shape
    pieces, cols = table.shape[0], grads[0].shape[1]
    return pl.pallas_call(
        weigh_near_kernel,
        out_shape=jax.ShapeDtypeStruct((pieces, width, cols), jnp.float32),
        grid_spec=pltpu.PrefetchScalarGridSpec(
            num_scalar_prefetch=1,
            grid=(pieces,),
            in_specs=[
                pl.BlockSpec(
                    (1, count, length, width), lambda piece, table: (2 * table[piece], 0, 0, 0)
                ),
                pl.BlockSpec(
                    (1, 1, length, width), lambda piece, table: (2 * table[piece] + 1, 0, 0, 0)
                ),
            ]
            + [pl.BlockSpec(grad.shape, lambda piece, table: (0, 0)) for grad in grads],
            out_specs=pl.BlockSpec((1, width, cols), lambda piece, table: (piece, 0, 0)),
        ),
        compiler_params=pltpu.CompilerParams(vmem_limit_bytes=SMALL_VMEM_BYTES),
        cost_estimate=pl.CostEstimate(
            flops=6 * pieces * length * width * cols,
            bytes_accessed=4 * count * length * (pieces * width + cols),
            transcendentals=0,
        ),
    )(table, shared, shared, *grads)


def weigh_far_kernel(table, partial, rows, far_up, far_down, top, bottom):
    half = far_up.shape[0]
    total = partial[0] + dot(rows[0, 0, :half], far_up[...], 0, 0)
    total = (total + dot(rows[0, 0, half:], far_down[...], 0, 0)).astype(jnp.bfloat16)
    half = top.shape[1]
    top[0], bottom[0] = total[:half], total[half:]


def weigh_far(table, partial, shared, grads, start, stop):
    _, _, length, width = shared.shape
    cols = partial.shape[2]
    half = (1, width // 2, cols)
    out = jax.ShapeDtypeStruct((stop - start,) + half[1:], jnp.bfloat16)
    return pl.pallas_call(
        weigh_far_kernel,
        out_shape=(out, out),
        grid_spec=pltpu.PrefetchScalarGridSpec(
            num_scalar_prefetch=1,
            grid=(stop - start,),
            in_specs=[
                pl.BlockSpec((1, width, cols), lambda piece, table: (start + piece, 0, 0)),
                pl.BlockSpec(
                    (1, 1, length, width),
                    lambda piece, table: (2 * table[start + piece] + 1, 1, 0, 0),
                ),
            ]
            + [pl.BlockSpec(grad.shape, lambda piece, table: (0, 0)) for grad in grads],
            out_specs=(pl.BlockSpec(half, lambda piece, table: (piece, 0, 0)),) * 2,
        ),
        compiler_params=pltpu.CompilerParams(vmem_limit_bytes=SMALL_VMEM_BYTES),
        cost_estimate=pl.CostEstimate(
            flops=2 * (stop - start) * length * width * cols,
            bytes_accessed=(stop - start) * width * (6 * cols + 4 * length),
            transcendentals=0,
        ),
    )(table, partial, shared, *grads)


def terms_kernel(top, bottom, weight, terms):
    half = top.shape[0]
    terms[:half] = dot(top[...], weight[...], 1, 1).astype(jnp.bfloat16)
    terms[half:] = dot(bottom[...], weight[...], 1, 1).astype(jnp.bfloat16)


def row_terms(grads, weight):
    half = grads[0].shape
    rows = 2 * half[0]
    depth, cols = weight.shape
    width = depth // 8
    return pl.pallas_call(
        terms_kernel,
        out_shape=jax.ShapeDtypeStruct((rows, depth), jnp.bfloat16),
        grid=(depth // width,),
        in_specs=[
            pl.BlockSpec(half, lambda block: (0, 0)),
            pl.BlockSpec(half, lambda block: (0, 0)),
            pl.BlockSpec((width, cols), lambda block: (block, 0)),
        ],
        out_specs=pl.BlockSpec((rows, width), lambda block: (0, block)),
        compiler_params=pltpu.CompilerParams(vmem_limit_bytes=VMEM_BYTES),
        cost_estimate=pl.CostEstimate(
            flops=2 * rows * depth * cols,
            bytes_accessed=2 * (rows * cols + depth * (cols + rows)),
            transcendentals=0,
        ),
    )(*grads, weight)


def total_of(*terms):
    return sum(term.astype(jnp.float32) for term in terms).astype(jnp.bfloat16)


def ring_near(block, send):
    return send(block, 1), send(block, -1)


def ring_far(before, after, send):
    half = before.shape[0] // 2
    return send(before[:half], 1), send(after[half:], -1)


def shards(loader_rows, packing, segment_ids, qkv_weight, gain_query, gain_key, out_grad):
    owners = lax.axis_size("row")
    block_count, block_rows, feature_cols = loader_rows.shape
    weight_panel = lax.all_gather(qkv_weight, "row", axis=0, tiled=True)

    col, row = lax.axis_index("col"), lax.axis_index("row")
    y, core = col // 2, col % 2
    x, z = row // N_RING, row % N_RING
    outgoing = pack_blocks(packing, loader_rows, owners)
    arrived = lax.all_to_all(outgoing, "row", split_axis=0, concat_axis=0, tiled=True)
    own_rows = place_blocks(arrived, block_count)
    own_rows = own_rows.reshape(block_count * block_rows, feature_cols)

    half = feature_cols // 2
    left, right = own_rows[:, :half], own_rows[:, half:]
    same, change = jnp.where(z % 2 == 0, left, right), jnp.where(z % 2 == 0, right, left)
    near = ring_near(own_rows, send_y)
    share = [share_z(change, True), share_z(same, False)]
    near, share = lax.optimization_barrier((near, share))

    far = jnp.concatenate(ring_far(*near, send_y), axis=0)
    far, share = lax.optimization_barrier((far, jnp.stack(share)))
    own = jnp.stack([own_rows, *near, far])
    other = swap_core(own)
    shared = lax.all_gather(share, "col", axis=0)

    offsets = jnp.array([0, -1, 1, 2], jnp.int32)
    ys = (y + offsets) % N_RING
    order = jnp.concatenate([ys * 2 + core, ys * 2 + 1 - core]).astype(jnp.int32)
    table = ((x - offsets) % N_RING).astype(jnp.int32)
    attn_out, top, bottom = run_heads(
        order, own, other, weight_panel, gain_query, gain_key, segment_ids[0], out_grad
    )

    before_top, after_bottom = send_z(top, 1), send_z(bottom, -1)
    before_bottom, after_top = send_z(bottom, 1), send_z(top, -1)
    near, row_sums = lax.optimization_barrier(
        (
            [before_top, before_bottom, after_top, after_bottom],
            row_terms((top, bottom), weight_panel),
        )
    )
    far, partial = lax.optimization_barrier(
        (
            (send_z(before_top, 1), send_z(after_bottom, -1)),
            weigh_near(table, shared, [top, bottom, *near]),
        )
    )
    tops, bottoms = weigh_far(table, partial, shared, far, 3, 4)
    up, down = send_x(tops[0], 1), send_x(bottoms[0], -1)
    tops, bottoms = weigh_far(table, partial, shared, far, 0, 3)
    after = jnp.concatenate([total_of(tops[1], up), bottoms[1]], axis=0)
    before = jnp.concatenate([tops[2], total_of(bottoms[2], down)], axis=0)
    here = jnp.concatenate([tops[0], bottoms[0]], axis=0)
    grad_weight = total_of(here, send_x(after, 1), send_x(before, -1))
    grad_rows = lax.psum_scatter(row_sums, "col", scatter_dimension=1, tiled=True)
    return (attn_out, grad_rows, grad_weight)


def solution(mesh):
    in_specs = (
        P("row", None, "col"),
        P("row"),
        P("row", None),
        P("row", "col"),
        P("col", None),
        P("col", None),
        P("row", "col"),
    )
    out_specs = (P("row", "col"), P("row", "col"), P("row", "col"))
    return jax.shard_map(shards, mesh=mesh, in_specs=in_specs, out_specs=out_specs, check_vma=False)
```
